256 devices in a mesh: table: 32 (over x, y, core), group: 8 (over z).
Axes of the slice: x: 4, y: 4, z: 8, core: 2. Of those that a mesh axis runs over, the one named last changes fastest.
Arguments:
- table: bfloat16 [32768, 512], P('table'), may hold values from -6 to 6
- fetch_rows: int32 [256, 32, 8], P(('table', 'group')), may hold values from 0 to 1023, as said below
- item_slot: int32 [65536], P(('table', 'group')), may hold values from 0 to 255, as said below
- seq_lengths: int32 [256, 8], P(('table', 'group')), may hold values from 1 to 128, 256 in all within a row
- w_in: bfloat16 [512, 2048], replicated, may hold values from -0.25 to 0.25
- w_out: bfloat16 [512, 512], replicated, may hold values from -0.25 to 0.25
- out_cot: bfloat16 [65536, 512], P(('table', 'group')), may hold values from -6 to 6
Outputs:
- layer_out: bfloat16 [65536, 512], P(('table', 'group'))
- table_grad: bfloat16 [8, 32768, 512], P('group', 'table')
- w_in_grad: float32 [512, 2048], replicated
- w_out_grad: float32 [512, 512], replicated
The draws below stay inside these ranges and needn't reach their ends.
Inputs may be any that keep to these rules, and one draw needn't show every extreme that they name: `fetch_rows`: the 8 entries of one shard's list for one owner are distinct rows of that owner's shard. `item_slot`: entry c of a shard's list for owner o is slot o * 8 + c. In each group, for one owner drawn from the seed, every shard names all 8 entries of its list for that owner.
All inputs are finite; a program needn't handle non-finite values.
Results may differ from the reference program's by a relative error of at most 0.019.
Values may be sent and summed in bfloat16 or wider, within the bound.
A program may use at most 64 MiB of HBM per device.

```python
import math
import jax
import jax.numpy as jnp
import numpy as np
from jax import lax

D = 512
HEADS = 8
TOK_DEV = 256
ROWS_DEV = 1024
SEQS_DEV = 8
LEN_MAX = 128
CAP = 8
SHARDS = 256
TOKENS = 65536
ROWS = 32768
N_TABLE = 32
N_GROUP = 8


def shared_layout(key):
    count_key, owner_key, order_key = jax.random.split(key, 3)
    counts = jax.random.randint(count_key, (SHARDS, N_TABLE), 1, CAP + 1)
    hot_owner = jax.random.randint(owner_key, (N_GROUP,), 0, N_TABLE)
    shard_group = jnp.arange(SHARDS) % N_GROUP
    owners = jnp.arange(N_TABLE)
    counts = jnp.where(owners[None, :] == hot_owner[shard_group][:, None], CAP, counts)
    scores = jax.random.randint(order_key, (SHARDS, N_TABLE, CAP), 0, 65536) * CAP + jnp.arange(CAP)
    ranks = jnp.argsort(jnp.argsort(scores, axis=-1), axis=-1)
    used_slots = ranks < counts[:, :, None]
    return (ranks, used_slots)


def draw_fetch_rows(key, part):
    ranks, used_slots = shared_layout(key)
    key = jax.random.fold_in(key, 11)
    base_key, jitter_key = jax.random.split(key)
    stride = ROWS_DEV // CAP
    offsets = jax.random.randint(base_key, (SHARDS, N_TABLE, 1), 0, ROWS_DEV)
    jitter = jax.random.randint(jitter_key, (SHARDS, N_TABLE, CAP), 0, stride)
    return ((offsets + ranks * stride + jitter) % ROWS_DEV).astype(jnp.int32)


def draw_item_slot(key, part):
    ranks, used_slots = shared_layout(key)
    key = jax.random.fold_in(key, 23)
    extra_key, order_key = jax.random.split(key)
    slot_total = N_TABLE * CAP
    flat_used = used_slots.reshape(SHARDS, slot_total)
    slot_numbers = jnp.arange(slot_total)
    listed = jnp.argsort(jnp.where(flat_used, 0, slot_total) + slot_numbers[None, :], axis=-1)
    live_count = jnp.sum(flat_used.astype(jnp.int32), axis=-1)
    positions = jnp.arange(TOK_DEV)
    extra = jax.random.randint(extra_key, (SHARDS, TOK_DEV), 0, live_count[:, None])
    picked = jnp.where(positions[None, :] < live_count[:, None], positions[None, :], extra)
    chosen = jnp.take_along_axis(listed, picked, axis=-1)
    scores = jax.random.randint(order_key, (SHARDS, TOK_DEV), 0, 65536) * TOK_DEV + positions[None, :]
    shuffle = jnp.argsort(scores, axis=-1)
    return jnp.take_along_axis(chosen, shuffle, axis=-1).reshape(TOKENS).astype(jnp.int32)


def steps_of(rng, dims, cuts, least, high):
    factor_of = 1.0
    for dim, parts in cuts:
        heights = jax.random.uniform(jax.random.fold_in(jax.random.fold_in(rng, 6), dim), (parts,), jnp.float32, least / len(cuts), high / len(cuts))
        factor_of = factor_of * jnp.repeat(jnp.exp(heights), dims[dim] // parts).reshape((-1,) + (1,) * (len(dims) - 1 - dim))
    return factor_of


def profile(number_of, total, most, slope):
    weights = [(1 << 20) // math.isqrt(standing ** slope) + 1 for standing in range(2, number_of + 1)]
    rest, given = total - most - (number_of - 1), [1] * (number_of - 1)
    while rest > 0:
        candidates = [i for i in range(number_of - 1) if given[i] < most]
        mass, budget = sum([weights[i] for i in candidates]), rest
        for i in candidates:
            more = min(most - given[i], max(1, budget * weights[i] // mass), rest)
            given[i] = given[i] + more
            rest = rest - more
    return np.array([most] + given)


def uneven(key, amount, total, reach, slope):
    if amount == 2:
        one = jax.random.randint(key, (), max(1, total - reach), min(reach, total - 1) + 1)
        return jnp.stack([one, total - one])
    tallies = jnp.asarray(profile(amount, total, reach, slope), jnp.int32)
    couples = (amount - 1) // 2
    giver, sink = tallies[1:1 + 2 * couples:2], tallies[2:2 + 2 * couples:2]
    room = jnp.minimum(giver - 1, reach - sink)
    passed = jax.random.randint(jax.random.fold_in(key, 1), (couples,), 0, 1 << 20) % (room + 1)
    tallies = tallies.at[1:1 + 2 * couples:2].set(giver - passed).at[2:2 + 2 * couples:2].set(sink + passed)
    return tallies[jax.random.permutation(jax.random.fold_in(key, 2), amount)]


def normal_values(key, shape, deviation, bound, cuts=(), kind=jnp.bfloat16):
    drawn = jax.random.normal(key, shape, jnp.float32) * deviation
    if len(cuts) > 0:
        drawn = steps_of(key, shape, cuts, -0.22, 0.18) * drawn
    return jnp.clip(drawn, min=-bound, max=bound).astype(kind)


def setup_inputs(seed: int = 0) -> dict:
    splits = jax.random.split(jax.random.key(seed), 8)
    return {
        "table": normal_values(splits[0], (ROWS, D), 1.0, 6.0, ((0, 32),)),
        "fetch_rows": draw_fetch_rows(jax.random.fold_in(splits[7], 71), 0),
        "item_slot": draw_item_slot(jax.random.fold_in(splits[7], 71), 0),
        "seq_lengths": jax.vmap(lambda own: uneven(own, SEQS_DEV, TOK_DEV, LEN_MAX, 1))(jax.random.split(splits[3], SHARDS)).reshape((SHARDS, SEQS_DEV)).astype(jnp.int32),
        "w_in": normal_values(splits[4], (D, 4 * D), D ** -0.5, 0.25),
        "w_out": normal_values(splits[5], (D, D), D ** -0.5, 0.25),
        "out_cot": normal_values(splits[6], (TOKENS, D), 1.0, 6.0, ((0, 256),)),
    }


EPS = 1e-05

def normalize(values):
    row_mean = lax.optimization_barrier(jnp.mean(values, axis=-1, keepdims=True))
    centred = values - row_mean
    spread = lax.optimization_barrier(jnp.mean(centred * centred, axis=-1, keepdims=True))
    return centred * lax.rsqrt(spread + EPS)

def segment_ids(lengths, token_count):
    sequence_ends = jnp.cumsum(lengths.astype(jnp.int32)).astype(jnp.int32)
    positions = jnp.arange(token_count, dtype=jnp.int32)
    return lax.optimization_barrier(jnp.sum((positions[:, None] >= sequence_ends[None, :]).astype(jnp.int32), axis=1)).astype(jnp.int32)

def hstu_layer(embedded, w_in, w_out, segment):
    token_count, width = embedded.shape
    head_dim = width // HEADS
    block_rows = min(512, token_count)
    inputs32 = embedded.astype(jnp.float32)
    normed = normalize(inputs32).astype(jnp.bfloat16)
    projected = jax.nn.silu(jnp.dot(normed, w_in, preferred_element_type=jnp.float32)).astype(jnp.bfloat16)
    gate_u = projected[:, :width]
    value_heads = projected[:, width:2 * width].reshape(token_count, HEADS, head_dim)
    queries = projected[:, 2 * width:3 * width].reshape(token_count, HEADS, head_dim)
    key_heads = projected[:, 3 * width:].reshape(token_count, HEADS, head_dim)
    score_scale = head_dim ** (-0.5)
    positions = jnp.arange(token_count, dtype=jnp.int32)
    pieces = []
    for block_index in range(token_count // block_rows):
        first_row = block_index * block_rows
        last_row = first_row + block_rows
        scores = jnp.einsum('qhd,khd->hqk', queries[first_row:last_row].astype(jnp.float32), key_heads[:last_row].astype(jnp.float32)) * score_scale
        allowed = (segment[first_row:last_row, None] == segment[None, :last_row]) & (positions[first_row:last_row, None] >= positions[None, :last_row])
        weights = jnp.where(allowed[None], jax.nn.silu(scores), 0.0).astype(jnp.bfloat16)
        mixed_block = jnp.einsum('hqk,khd->qhd', weights.astype(jnp.float32), value_heads[:last_row].astype(jnp.float32))
        pieces.append(mixed_block.reshape(block_rows, width))
    mixed = jnp.concatenate(pieces, axis=0)
    gated = (normalize(mixed) * gate_u.astype(jnp.float32)).astype(jnp.bfloat16)
    return (inputs32 + jnp.dot(gated, w_out, preferred_element_type=jnp.float32)).astype(jnp.bfloat16)

def reference(table, fetch_rows, item_slot, seq_lengths, w_in, w_out, out_cot):
    owner_base = jnp.arange(N_TABLE, dtype=jnp.int32)[None, :, None] * ROWS_DEV
    row_lists = (owner_base + fetch_rows).reshape(SHARDS, N_TABLE * CAP).astype(jnp.int32)
    token_slots = item_slot.reshape(SHARDS, TOK_DEV)
    cotangents = out_cot.reshape(SHARDS, TOK_DEV, D)

    def per_shard(totals, shard_inputs):
        row_list, slots_here, lengths, cotangent = shard_inputs
        embedded = table[row_list[slots_here]]
        segment = segment_ids(lengths, TOK_DEV)

        def layer(emb_rows, weight_in, weight_out):
            return hstu_layer(emb_rows, weight_in, weight_out, segment)
        shard_out, backward = jax.vjp(layer, embedded, w_in, w_out)
        d_embedded, grad_in, grad_out = backward(cotangent)
        slot_grad = jax.ops.segment_sum(d_embedded.astype(jnp.float32), slots_here, num_segments=N_TABLE * CAP).astype(jnp.bfloat16)
        totals = (totals[0] + grad_in.astype(jnp.float32), totals[1] + grad_out.astype(jnp.float32))
        return (totals, (shard_out, slot_grad))
    start_totals = (jnp.zeros((D, 4 * D), jnp.float32), jnp.zeros((D, D), jnp.float32))
    totals, (shard_outs, slot_grads) = lax.scan(per_shard, start_totals, (row_lists, token_slots, seq_lengths, cotangents))
    shard_group = (jnp.arange(SHARDS, dtype=jnp.int32) % N_GROUP)[:, None]
    targets = (shard_group * ROWS + row_lists).reshape(-1).astype(jnp.int32)
    summed = jax.ops.segment_sum(slot_grads.astype(jnp.float32).reshape(-1, D), targets, num_segments=N_GROUP * ROWS)
    table_grad = summed.reshape(N_GROUP, ROWS, D).astype(jnp.bfloat16)
    grad_scale = float(TOKENS) ** (-0.5)
    layer_out = shard_outs.reshape(TOKENS, D)
    return (layer_out, table_grad, totals[0] * grad_scale, totals[1] * grad_scale)
```

```python
import functools
import math

import jax
import jax.numpy as jnp
from jax import lax
from jax.experimental import pallas as pl
from jax.experimental.pallas import tpu as pltpu
from jax.sharding import PartitionSpec as P

HEADS = 8
EPS = 1e-05
MESH = pl.DeviceIdType.MESH
BF = jnp.bfloat16
F32 = jnp.float32

NN = (((1,), (0,)), ((), ()))
NT = (((1,), (1,)), ((), ()))
TN = (((0,), (0,)), ((), ()))


def mm(a, b, dims=NN):
    return lax.dot_general(a, b, dims, preferred_element_type=F32)


def rows_of(start, size):
    return pl.ds(pl.multiple_of(start, size), size)


def kernel(
    n, nz, count, cap, rows, tokens, width,
    fetch_ref, slot_ref, len_ref, table_hbm, win_hbm, wout_hbm, cot_hbm,
    out_ref, tg_ref, full_ref, fullo_ref,
    table_v, win_v, wout_v, cot_v,
    req_s, req_r, found, rows_r, sg_s, sg_r,
    emb, n32, normed, proj, dsil, dpre, weights, dfac, mixed, allowed,
    g, pr, h, r1, s1, r2, s2, r3, a2,
    ro1, ro2, so2, ro3,
    load_sem, send_sem, recv_sem,
):
    t = lax.axis_index("table")
    z = lax.axis_index("group")
    x = lax.div(t, 2 * n)
    y = lax.rem(lax.div(t, 2), n)
    c = lax.rem(t, 2)
    slots = count * cap
    half = width // 2
    R0 = width // 2
    R1 = R0 // n
    R2 = R1 // n
    CZ = 4 * width // nz

    def at(px, py, pc):
        return (px * n + py) * 2 + pc

    def plus(v, d, m):
        return lax.rem(v + d, m)

    offsets = [(dx, dy, dc) for dx in range(n) for dy in range(n) for dc in range(2)][1:]
    ahead = [at(plus(x, dx, n), plus(y, dy, n), plus(c, dc, 2)) for dx, dy, dc in offsets]
    behind = [at(plus(x, n - dx, n), plus(y, n - dy, n), plus(c, 2 - dc, 2)) for dx, dy, dc in offsets]
    zs = [plus(z, d, nz) for d in range(1, nz)]
    xs = [at(plus(x, d, n), y, c) for d in range(1, n)]
    ys = [at(x, plus(y, d, n), c) for d in range(1, n)]
    partner = at(x, y, 1 - c)

    loads = [
        pltpu.make_async_copy(src, dst, load_sem.at[i])
        for i, (src, dst) in enumerate(
            ((table_hbm, table_v), (win_hbm, win_v), (wout_hbm, wout_v), (cot_hbm, cot_v))
        )
    ]
    for copy in loads:
        copy.start()

    barrier = pltpu.get_barrier_semaphore()
    for peer in ahead:
        pl.semaphore_signal(barrier, inc=1, device_id=(peer, z), device_id_type=MESH)
    for peer in zs:
        pl.semaphore_signal(barrier, inc=1, device_id=(t, peer), device_id_type=MESH)

    names = {}
    pending = []

    def sem(name):
        return names.setdefault(name, len(names))

    def send(src, dst, to, name):
        i = sem(name)
        pltpu.make_async_remote_copy(
            src_ref=src, dst_ref=dst, send_sem=send_sem.at[i], recv_sem=recv_sem.at[i],
            device_id=to, device_id_type=MESH,
        ).start()

    def arrived(ref, name):
        pltpu.make_async_copy(ref, ref, recv_sem.at[sem(name)]).wait()
        pending.append((ref, name))

    for o in range(count):
        for e in range(cap):
            req_s[o, e : e + 1, :] = jnp.full((1, 128), fetch_ref[o, e], jnp.int32)
    pl.semaphore_wait(barrier, count - 1 + nz - 1)
    for k, peer in enumerate(ahead):
        send(req_s.at[peer], req_r.at[k], (peer, z), "list")
    req_r[count - 1] = req_s[t]

    ends = []
    total = jnp.int32(0)
    for s in range(len_ref.shape[1]):
        total = total + len_ref[0, s]
        ends.append(total)
    pos_i = lax.broadcasted_iota(jnp.int32, (tokens, tokens), 0)
    pos_j = lax.broadcasted_iota(jnp.int32, (tokens, tokens), 1)
    first = jnp.zeros((tokens, tokens), jnp.int32)
    for e in ends:
        first = jnp.where(pos_i >= e, e, first)
    allowed[...] = jnp.where((pos_j >= first) & (pos_j <= pos_i), 1.0, 0.0).astype(F32)
    slot_hot = jnp.where(
        lax.broadcasted_iota(jnp.int32, (slots, tokens), 0) == slot_ref[...], 1.0, 0.0
    ).astype(BF)

    arrived(req_r.at[pl.ds(0, count - 1)], "list")
    loads[0].wait()
    lane = lax.broadcasted_iota(jnp.int32, (slots, 128), 1)
    wanted = req_r[...].reshape(slots, 128)
    row_hot = jnp.concatenate(
        [jnp.where(wanted == lane + 128 * i, 1.0, 0.0).astype(BF) for i in range(rows // 128)], axis=1
    )

    def packed(ref, lo, hi):
        ref[...] = jnp.concatenate(
            [lo.reshape(count, cap, half), hi.reshape(count, cap, half)], axis=1
        ).astype(BF)

    def unpacked(ref):
        v = ref[...].astype(F32)
        return jnp.concatenate(
            [v[:, :cap].reshape(slots, half), v[:, cap:].reshape(slots, half)], axis=1
        ).astype(BF)

    packed(found, mm(row_hot, table_v[:, :half]), mm(row_hot, table_v[:, half:]))
    for k, peer in enumerate(behind):
        send(found.at[k], rows_r.at[t], (peer, z), "rows")
    rows_r[t] = found[count - 1]
    loads[1].wait()
    loads[2].wait()
    loads[3].wait()
    arrived(rows_r.at[pl.ds(0, count - 1)], "rows")

    e32 = mm(slot_hot, unpacked(rows_r), TN)
    emb[...] = e32
    cen = e32 - jnp.mean(e32, axis=1, keepdims=True)
    inv_e = lax.rsqrt(jnp.mean(cen * cen, axis=1, keepdims=True) + EPS)
    n32[...] = cen * inv_e
    normed[...] = n32[...].astype(BF)

    def cols(b):
        return slice(b * width, (b + 1) * width)

    for b in range(4):
        p = mm(normed[...], win_v[:, cols(b)])
        sg = jax.nn.sigmoid(p)
        proj[:, cols(b)] = (p * sg).astype(BF)
        dsil[:, cols(b)] = sg * (1.0 + p * (1.0 - sg))

    lanes = lax.broadcasted_iota(jnp.int32, (1, 128), 1)
    side = [
        jnp.where(lanes < 64, 1.0, 0.0).astype(BF),
        jnp.where(lanes >= 64, 1.0, 0.0).astype(BF),
    ]

    def pair(b, i):
        return proj[:, b * width + 128 * i : b * width + 128 * (i + 1)]

    scale = (width // HEADS) ** -0.5
    for i in range(HEADS // 2):
        q, k, v = pair(2, i), pair(3, i), pair(1, i)
        part = None
        for j in range(2):
            s = mm(q, k * side[j], NT) * scale
            sg = jax.nn.sigmoid(s)
            keep = allowed[...]
            w = (keep * (s * sg)).astype(BF)
            weights[2 * i + j] = w
            dfac[2 * i + j] = (keep * scale) * (sg * (1.0 + s * (1.0 - sg)))
            term = mm(w, v * side[j])
            part = term if part is None else part + term
        mixed[:, 128 * i : 128 * (i + 1)] = part

    m32 = mixed[...]
    cen = m32 - jnp.mean(m32, axis=1, keepdims=True)
    inv_m = lax.rsqrt(jnp.mean(cen * cen, axis=1, keepdims=True) + EPS)
    nm = cen * inv_m
    u32 = proj[:, cols(0)].astype(F32)
    gated = (nm * u32).astype(BF)
    cot = cot_v[...]
    out_ref[...] = (emb[...] + mm(gated, wout_v[...])).astype(BF)

    own = rows_of(c * R0, R0)
    other = rows_of((1 - c) * R0, R0)

    def to_partner(b):
        send(g.at[b, other], pr.at[b], (partner, z), f"pair{b}")

    def first_peers(b):
        return (xs, x, ys, y) if b % 2 == 0 else (ys, y, xs, x)

    def plane(v, peers):
        return [plus(v, d, n) for d in range(1, n)]

    def pair_sum(b):
        arrived(pr.at[b], f"pair{b}")
        h[b] = (g[b, own].astype(F32) + pr[b].astype(F32)).astype(BF)
        if b < 4:
            peers, v, _, _ = first_peers(b)
            for k, (peer, place) in enumerate(zip(peers, plane(v, peers))):
                send(h.at[b, rows_of(place * R1, R1)], r1.at[b, k], (peer, z), f"first{b}")
        else:
            for k, place in enumerate(zs):
                send(h.at[b, rows_of(place * (R0 // nz), R0 // nz)], ro1.at[k], (t, place), "o_z")

    def first_sum(b):
        arrived(r1.at[b], f"first{b}")
        _, v, peers, w = first_peers(b)
        acc = h[b, rows_of(v * R1, R1)].astype(F32)
        for k in range(n - 1):
            acc = acc + r1[b, k].astype(F32)
        s1[b] = acc.astype(BF)
        for k, (peer, place) in enumerate(zip(peers, plane(w, peers))):
            send(s1.at[b, rows_of(place * R2, R2)], r2.at[b, k], (peer, z), f"second{b}")

    def second_sum(b):
        arrived(r2.at[b], f"second{b}")
        _, _, _, w = first_peers(b)
        acc = s1[b, rows_of(w * R2, R2)].astype(F32)
        for k in range(n - 1):
            acc = acc + r2[b, k].astype(F32)
        s2[:, cols(b)] = acc.astype(BF)

    d_gated = mm(cot, wout_v[...], NT).astype(BF).astype(F32)
    g[4] = mm(gated, cot, TN).astype(BF)
    to_partner(4)
    normed_t = normed[...].T

    def weight_grad(b, d_proj):
        d = (d_proj.astype(BF).astype(F32) * dsil[:, cols(b)]).astype(BF)
        dpre[:, cols(b)] = d
        g[b] = mm(normed_t, d).astype(BF)
        to_partner(b)

    weight_grad(0, d_gated * nm)
    pair_sum(4)

    gn = d_gated * u32
    dm = inv_m * (
        gn - jnp.mean(gn, axis=1, keepdims=True) - nm * jnp.mean(gn * nm, axis=1, keepdims=True)
    )
    mixed[...] = dm
    d_v = []
    for i in range(HEADS // 2):
        dm_i = mixed[:, 128 * i : 128 * (i + 1)].astype(BF)
        part = None
        for j in range(2):
            term = mm(weights[2 * i + j], dm_i * side[j], TN)
            part = term if part is None else part + term
        d_v.append(part)
    weight_grad(1, jnp.concatenate(d_v, axis=1))
    pair_sum(0)

    d_q, d_k = [], []
    for i in range(HEADS // 2):
        q, k, v = pair(2, i), pair(3, i), pair(1, i)
        dm_i = mixed[:, 128 * i : 128 * (i + 1)].astype(BF)
        part_q = part_k = None
        for j in range(2):
            dw = mm(dm_i, v * side[j], NT).astype(BF).astype(F32)
            ds = (dw * dfac[2 * i + j]).astype(BF)
            term_q = mm(ds, k * side[j])
            term_k = mm(ds, q * side[j], TN)
            part_q = term_q if part_q is None else part_q + term_q
            part_k = term_k if part_k is None else part_k + term_k
        d_q.append(part_q)
        d_k.append(part_k)
    weight_grad(2, jnp.concatenate(d_q, axis=1))
    weight_grad(3, jnp.concatenate(d_k, axis=1))
    pair_sum(1)
    pair_sum(2)
    pair_sum(3)

    dn = mm(dpre[...], win_v[...], NT).astype(BF).astype(F32)
    first_sum(0)
    first_sum(1)
    nv = n32[...]
    de = cot.astype(F32) + inv_e * (
        dn - jnp.mean(dn, axis=1, keepdims=True) - nv * jnp.mean(dn * nv, axis=1, keepdims=True)
    )
    sg32 = mm(slot_hot, de.astype(BF))
    packed(sg_s, sg32[:, :half], sg32[:, half:])
    for k, peer in enumerate(ahead):
        send(sg_s.at[peer], sg_r.at[k], (peer, z), "slot")
    sg_r[count - 1] = sg_s[t]

    RZ = R0 // nz
    CX = width // n
    arrived(ro1, "o_z")
    acc = h[4, rows_of(z * RZ, RZ)].astype(F32)
    for k in range(nz - 1):
        acc = acc + ro1[k].astype(F32)
    h[4, rows_of(z * RZ, RZ)] = acc.astype(BF)
    for k, (peer, place) in enumerate(zip(xs, plane(x, xs))):
        send(
            h.at[4, rows_of(z * RZ, RZ), rows_of(place * CX, CX)], ro2.at[k], (peer, z), "o_x"
        )
    first_sum(2)
    first_sum(3)
    arrived(ro2, "o_x")
    acc = h[4, rows_of(z * RZ, RZ), rows_of(x * CX, CX)].astype(F32)
    for k in range(n - 1):
        acc = acc + ro2[k].astype(F32)
    so2[...] = acc.astype(BF)
    ro3[y] = so2[...]
    for peer in ys:
        send(so2, ro3.at[y], (peer, z), "o_y")
    for b in range(4):
        second_sum(b)

    for k, place in enumerate(zs):
        send(s2.at[:, rows_of(place * CZ, CZ)], r3.at[k], (t, place), "last")

    arrived(sg_r.at[pl.ds(0, count - 1)], "slot")
    tg_ref[...] = mm(row_hot, unpacked(sg_r), TN).astype(BF)

    arrived(ro3.at[pl.ds(0, n - 1)], "o_y")
    acc = ro3[0].astype(F32)
    for k in range(1, n):
        acc = acc + ro3[k].astype(F32)
    orow = c * R0 + z * RZ
    ocol = rows_of(x * CX, CX)
    fullo_ref[rows_of(orow, RZ), ocol] = acc.astype(BF)
    for peer in xs:
        strip = fullo_ref.at[rows_of(orow, RZ), ocol]
        send(strip, strip, (peer, z), "o_gx")

    arrived(r3, "last")
    zcols = rows_of(z * CZ, CZ)
    acc = s2[:, zcols].astype(F32)
    for k in range(nz - 1):
        acc = acc + r3[k].astype(F32)
    a2[:, zcols] = acc.astype(BF)
    for peer in zs:
        send(a2.at[:, zcols], a2.at[:, zcols], (t, peer), "g_z")

    arrived(ro2, "o_gx")
    for peer in zs:
        strip = fullo_ref.at[rows_of(orow, RZ)]
        send(strip, strip, (t, peer), "o_gz")

    arrived(a2.at[:, pl.ds(0, CZ * (nz - 1))], "g_z")
    strips = []
    for b in range(4):
        _, v, peers, w = first_peers(b)
        base = c * R0 + v * R1
        strips.append((base, v))
        mine = rows_of(base + w * R2, R2)
        full_ref[mine, cols(b)] = a2[:, cols(b)]
        for peer in peers:
            strip = full_ref.at[mine, cols(b)]
            send(strip, strip, (peer, z), f"g_second{b}")
    arrived(ro1, "o_gz")
    strip = fullo_ref.at[own]
    send(strip, strip, (partner, z), "o_gp")
    for b in range(4):
        arrived(r2.at[b], f"g_second{b}")
        peers, _, _, _ = first_peers(b)
        base, v = strips[b]
        strip = full_ref.at[rows_of(base, R1), cols(b)]
        for k, peer in enumerate(peers):
            send(strip, strip, (peer, z), f"g_first{b}_{k}")
        send(strip, strip, (partner, z), f"g_pair{b}_{n - 1}")
    for k in range(n - 1):
        for b in range(4):
            arrived(s1.at[b], f"g_first{b}_{k}")
            _, v, _, _ = first_peers(b)
            place = plus(v, n - 1 - k, n)
            strip = full_ref.at[rows_of(c * R0 + place * R1, R1), cols(b)]
            send(strip, strip, (partner, z), f"g_pair{b}_{k}")
    arrived(fullo_ref.at[other], "o_gp")
    for k in range(n):
        for b in range(4):
            arrived(s1.at[b], f"g_pair{b}_{(k + n - 1) % n}")

    for ref, name in pending:
        pltpu.make_async_copy(ref, ref, send_sem.at[sem(name)]).wait()
    assert len(names) <= send_sem.shape[0]


def body(n, nz, table, fetch_rows, item_slot, seq_lengths, w_in, w_out, out_cot):
    _, count, cap = fetch_rows.shape
    rows, width = table.shape
    tokens = item_slot.shape[0]
    slots = count * cap
    half = width // 2
    R0 = width // 2
    R1 = R0 // n
    R2 = R1 // n
    CZ = 4 * width // nz
    any_ = pl.BlockSpec(memory_space=pl.ANY)
    vmem = pl.BlockSpec(memory_space=pltpu.VMEM)
    smem = pl.BlockSpec(memory_space=pltpu.SMEM)
    V = pltpu.VMEM
    layer_out, table_grad, sum_in, sum_out = pl.pallas_call(
        functools.partial(kernel, n, nz, count, cap, rows, tokens, width),
        out_shape=(
            jax.ShapeDtypeStruct((tokens, width), BF),
            jax.ShapeDtypeStruct((rows, width), BF),
            jax.ShapeDtypeStruct((width, 4 * width), BF),
            jax.ShapeDtypeStruct((width, width), BF),
        ),
        in_specs=[smem, vmem, smem, any_, any_, any_, any_],
        out_specs=(vmem, vmem, vmem, vmem),
        scratch_shapes=[
            V((rows, width), BF), V((width, 4 * width), BF), V((width, width), BF), V((tokens, width), BF),
            V((count, cap, 128), jnp.int32), V((count, cap, 128), jnp.int32),
            V((count, 2 * cap, half), BF), V((count, 2 * cap, half), BF),
            V((count, 2 * cap, half), BF), V((count, 2 * cap, half), BF),
            V((tokens, width), F32), V((tokens, width), F32), V((tokens, width), BF),
            V((tokens, 4 * width), BF), V((tokens, 4 * width), F32), V((tokens, 4 * width), BF),
            V((HEADS, tokens, tokens), BF), V((HEADS, tokens, tokens), F32),
            V((tokens, width), F32), V((tokens, tokens), F32),
            V((5, width, width), BF), V((5, R0, width), BF), V((5, R0, width), BF),
            V((4, n - 1, R1, width), BF), V((4, R1, width), BF),
            V((4, n - 1, R2, width), BF), V((R2, 4 * width), BF),
            V((nz - 1, R2, CZ), BF), V((R2, 4 * width), BF),
            V((nz - 1, R0 // nz, width), BF), V((n - 1, R0 // nz, width // n), BF),
            V((R0 // nz, width // n), BF), V((n, R0 // nz, width // n), BF),
            pltpu.SemaphoreType.DMA((4,)),
            pltpu.SemaphoreType.DMA((64,)),
            pltpu.SemaphoreType.DMA((64,)),
        ],
        compiler_params=pltpu.CompilerParams(
            collective_id=0, has_side_effects=True, vmem_limit_bytes=56 * 1024 * 1024
        ),
    )(
        fetch_rows.reshape(count, cap), item_slot.reshape(1, tokens), seq_lengths,
        table, w_in, w_out, out_cot,
    )
    grad_scale = float(tokens * count * nz) ** (-0.5)
    return (
        layer_out,
        table_grad[None],
        sum_in.astype(F32) * grad_scale,
        sum_out.astype(F32) * grad_scale,
    )


def solution(mesh):
    placed = (
        P("table", None),
        P(("table", "group"), None, None),
        P(("table", "group")),
        P(("table", "group"), None),
        P(),
        P(),
        P(("table", "group"), None),
    )
    n = math.isqrt(mesh.shape["table"] // 2)
    return jax.shard_map(
        functools.partial(body, n, mesh.shape["group"]),
        mesh=mesh,
        in_specs=placed,
        out_specs=(P(("table", "group"), None), P("group", "table", None), P(), P()),
        check_vma=False,
    )
```

```python
import functools
import math

import jax
import jax.numpy as jnp
from jax import lax
from jax.experimental import pallas as pl
from jax.experimental.pallas import tpu as pltpu
from jax.sharding import PartitionSpec as P

HEADS = 8
EPS = 1e-05
MESH = pl.DeviceIdType.MESH
BF = jnp.bfloat16
F32 = jnp.float32

NN = (((1,), (0,)), ((), ()))
NT = (((1,), (1,)), ((), ()))
TN = (((0,), (0,)), ((), ()))


def mm(a, b, dims=NN):
    return lax.dot_general(a, b, dims, preferred_element_type=F32)


def rows_of(start, size):
    return pl.ds(pl.multiple_of(start, size), size)


def kernel(
    n, nz, count, cap, rows, tokens, width, grad_scale,
    fetch_hbm, slot_hbm, len_hbm, table_hbm, win_hbm, wout_hbm, cot_hbm,
    out_ref, tg_ref, gin_ref, gout_ref,
    fetch_ref, slot_ref, len_ref, table_v, win_v, wout_v, cot_v,
    req_s, req_r, found, rows_r, sg_s, sg_r,
    row_hot, emb, n32, normed, proj, dsil, dpre, weights, dfac, mixed, allowed,
    g, pr, h, r1, s1, r2, s2, r3, a2,
    ro1, ro2, so2, ro3, full_ref, fullo_ref,
    load_sem, send_sem, recv_sem,
):
    t = lax.axis_index("table")
    z = lax.axis_index("group")
    x = lax.div(t, 2 * n)
    y = lax.rem(lax.div(t, 2), n)
    c = lax.rem(t, 2)
    slots = count * cap
    half = width // 2
    R0 = width // 2
    R1 = R0 // n
    R2 = R1 // n
    CZ = 2 * width // nz

    def at(px, py, pc):
        return (px * n + py) * 2 + pc

    def plus(v, d, m):
        return lax.rem(v + d, m)

    def far(d, m):
        return min(d, m - d)

    offsets = [(dx, dy, dc) for dx in range(n) for dy in range(n) for dc in range(2)][1:]
    offsets.sort(key=lambda o: (-far(o[0], n) - far(o[1], n), o))
    steps = sorted(range(1, n), key=lambda d: -far(d, n))
    zsteps = sorted(range(1, nz), key=lambda d: -far(d, nz))
    ahead = [at(plus(x, dx, n), plus(y, dy, n), plus(c, dc, 2)) for dx, dy, dc in offsets]
    behind = [at(plus(x, n - dx, n), plus(y, n - dy, n), plus(c, 2 - dc, 2)) for dx, dy, dc in offsets]
    zs = [plus(z, d, nz) for d in zsteps]
    xs = [at(plus(x, d, n), y, c) for d in steps]
    ys = [at(x, plus(y, d, n), c) for d in steps]
    partner = at(x, y, 1 - c)

    loads = [
        pltpu.make_async_copy(src, dst, load_sem.at[i])
        for i, (src, dst) in enumerate(
            (
                (fetch_hbm, fetch_ref), (len_hbm, len_ref), (slot_hbm, slot_ref),
                (table_hbm, table_v), (win_hbm, win_v), (wout_hbm, wout_v), (cot_hbm, cot_v),
            )
        )
    ]
    for copy in loads:
        copy.start()

    barrier = pltpu.get_barrier_semaphore()
    for peer in ahead:
        pl.semaphore_signal(barrier, inc=1, device_id=(peer, z), device_id_type=MESH)
    for peer in zs:
        pl.semaphore_signal(barrier, inc=1, device_id=(t, peer), device_id_type=MESH)

    names = {}
    pending = []

    def sem(name):
        return names.setdefault(name, len(names))

    def send(src, dst, to, name):
        i = sem(name)
        pltpu.make_async_remote_copy(
            src_ref=src, dst_ref=dst, send_sem=send_sem.at[i], recv_sem=recv_sem.at[i],
            device_id=to, device_id_type=MESH,
        ).start()

    def arrived(ref, name):
        pltpu.make_async_copy(ref, ref, recv_sem.at[sem(name)]).wait()
        pending.append((ref, name))

    loads[0].wait()
    lane = lax.broadcasted_iota(jnp.int32, (1, 128), 1)
    for o in range(count):
        line = jnp.zeros((1, 128), jnp.int32)
        for e in range(cap):
            line = jnp.where(lane == e, fetch_ref[e, o], line)
        req_s[o] = line
    pl.semaphore_wait(barrier, count - 1 + nz - 1)
    for k, peer in enumerate(ahead):
        send(req_s.at[peer], req_r.at[k], (peer, z), f"list{0 if k < count // 2 else count // 2}")
    req_r[count - 1] = req_s[t]

    loads[1].wait()
    loads[2].wait()
    ends = []
    total = jnp.int32(0)
    for s in range(len_ref.shape[1]):
        total = total + len_ref[0, s]
        ends.append(total)
    pos_i = lax.broadcasted_iota(jnp.int32, (tokens, tokens), 0)
    pos_j = lax.broadcasted_iota(jnp.int32, (tokens, tokens), 1)
    first = jnp.zeros((tokens, tokens), jnp.int32)
    for e in ends:
        first = jnp.where(pos_i >= e, e, first)
    allowed[...] = jnp.where((pos_j >= first) & (pos_j <= pos_i), 1.0, 0.0).astype(F32)
    slot_hot = jnp.where(
        lax.broadcasted_iota(jnp.int32, (slots, tokens), 0) == slot_ref[...], 1.0, 0.0
    ).astype(BF)

    def hot_rows(start, size):
        lists = jnp.broadcast_to(req_r[start : start + size].astype(F32), (size, cap, 128))
        diagonal = lax.broadcasted_iota(jnp.int32, (size, cap, 128), 1) == lax.broadcasted_iota(
            jnp.int32, (size, cap, 128), 2
        )
        wanted = jnp.sum(jnp.where(diagonal, lists, 0.0), axis=2, keepdims=True).reshape(size * cap, 1)
        lane = lax.broadcasted_iota(jnp.int32, (size * cap, 128), 1).astype(F32)
        row_hot[start * cap : (start + size) * cap] = jnp.concatenate(
            [jnp.where(wanted == lane + 128.0 * i, 1.0, 0.0).astype(BF) for i in range(rows // 128)], axis=1
        )

    def packed(lo, hi):
        return jnp.concatenate([lo.reshape(-1, cap, half), hi.reshape(-1, cap, half)], axis=1).astype(BF)

    def unpacked(ref):
        v = ref[...].astype(F32)
        return jnp.concatenate(
            [v[:, :cap].reshape(slots, half), v[:, cap:].reshape(slots, half)], axis=1
        ).astype(BF)

    cut = count // 2
    for start, size, got in ((cut, cut, cut - 1), (0, cut, cut)):
        arrived(req_r.at[pl.ds(start, got)], f"list{start}")
        if start:
            loads[3].wait()
        hot_rows(start, size)
        hot = row_hot[start * cap : (start + size) * cap]
        found[start : start + size] = packed(mm(hot, table_v[:, :half]), mm(hot, table_v[:, half:]))
        for k in range(start, start + got):
            send(found.at[k], rows_r.at[t], (behind[k], z), "rows")
    rows_r[t] = found[count - 1]
    for i in (4, 5, 6):
        loads[i].wait()
    arrived(rows_r.at[pl.ds(0, count - 1)], "rows")

    e32 = mm(slot_hot, unpacked(rows_r), TN)
    emb[...] = e32
    cen = e32 - jnp.mean(e32, axis=1, keepdims=True)
    inv_e = lax.rsqrt(jnp.mean(cen * cen, axis=1, keepdims=True) + EPS)
    n32[...] = cen * inv_e
    normed[...] = n32[...].astype(BF)

    def cols(b):
        return slice(b * width, (b + 1) * width)

    for b in range(4):
        p = mm(normed[...], win_v[:, cols(b)])
        sg = 0.5 + 0.5 * jnp.tanh(0.5 * p)
        proj[:, cols(b)] = (p * sg).astype(BF)
        dsil[:, cols(b)] = sg * (1.0 + p * (1.0 - sg))

    lanes = lax.broadcasted_iota(jnp.int32, (1, 128), 1)
    side = [
        jnp.where(lanes < 64, 1.0, 0.0).astype(BF),
        jnp.where(lanes >= 64, 1.0, 0.0).astype(BF),
    ]

    def pair(b, i):
        return proj[:, b * width + 128 * i : b * width + 128 * (i + 1)]

    scale = (width // HEADS) ** -0.5
    for i in range(HEADS // 2):
        q, k, v = pair(2, i), pair(3, i), pair(1, i)
        part = None
        for j in range(2):
            s = mm(q, k * side[j], NT) * scale
            sg = 0.5 + 0.5 * jnp.tanh(0.5 * s)
            keep = allowed[...]
            w = (keep * (s * sg)).astype(BF)
            weights[2 * i + j] = w
            dfac[2 * i + j] = (keep * scale) * (sg * (1.0 + s * (1.0 - sg)))
            term = mm(w, v * side[j])
            part = term if part is None else part + term
        mixed[:, 128 * i : 128 * (i + 1)] = part

    m32 = mixed[...]
    cen = m32 - jnp.mean(m32, axis=1, keepdims=True)
    inv_m = lax.rsqrt(jnp.mean(cen * cen, axis=1, keepdims=True) + EPS)
    nm = cen * inv_m
    u32 = proj[:, cols(0)].astype(F32)
    gated = (nm * u32).astype(BF)
    cot = cot_v[...]
    out_ref[...] = (emb[...] + mm(gated, wout_v[...])).astype(BF)

    own = rows_of(c * R0, R0)
    other = rows_of((1 - c) * R0, R0)

    def to_partner(b):
        send(g.at[b, other], pr.at[b], (partner, z), f"pair{b}")

    def first_peers(b):
        return (xs, x, ys, y) if b % 2 == 0 else (ys, y, xs, x)

    def plane(v, peers):
        return [plus(v, d, n) for d in steps]

    def pair_sum(b):
        arrived(pr.at[b], f"pair{b}")
        h[b] = (g[b, own].astype(F32) + pr[b].astype(F32)).astype(BF)
        if b < 4:
            peers, v, _, _ = first_peers(b)
            for k, (peer, place) in enumerate(zip(peers, plane(v, peers))):
                send(h.at[b, rows_of(place * R1, R1)], r1.at[b, k], (peer, z), f"first{b}")
        else:
            for k, place in enumerate(zs):
                send(h.at[b, rows_of(place * (R0 // nz), R0 // nz)], ro1.at[k], (t, place), "o_z")

    def first_sum(b):
        arrived(r1.at[b], f"first{b}")
        _, v, peers, w = first_peers(b)
        acc = h[b, rows_of(v * R1, R1)].astype(F32)
        for k in range(n - 1):
            acc = acc + r1[b, k].astype(F32)
        s1[b] = acc.astype(BF)
        for k, (peer, place) in enumerate(zip(peers, plane(w, peers))):
            send(s1.at[b, rows_of(place * R2, R2)], r2.at[b, k], (peer, z), f"second{b}")

    def second_sum(b):
        arrived(r2.at[b], f"second{b}")
        _, _, _, w = first_peers(b)
        acc = s1[b, rows_of(w * R2, R2)].astype(F32)
        for k in range(n - 1):
            acc = acc + r2[b, k].astype(F32)
        s2[b // 2, :, cols(b % 2)] = acc.astype(BF)
        if b % 2 == 1:
            for k, place in enumerate(zs):
                send(
                    s2.at[b // 2, :, rows_of(place * CZ, CZ)], r3.at[b // 2, k], (t, place), f"last{b // 2}"
                )

    zcols = rows_of(z * CZ, CZ)

    def last_sum(i):
        arrived(r3.at[i], f"last{i}")
        acc = s2[i, :, zcols].astype(F32)
        for k in range(nz - 1):
            acc = acc + r3[i, k].astype(F32)
        a2[i, :, zcols] = acc.astype(BF)
        for peer in zs:
            send(a2.at[i, :, zcols], a2.at[i, :, zcols], (t, peer), f"g_z{i}")

    def back_z(i):
        arrived(a2.at[i, :, pl.ds(0, CZ * (nz - 1))], f"g_z{i}")
        for b in (2 * i, 2 * i + 1):
            _, v, peers, w = first_peers(b)
            mine = rows_of(c * R0 + v * R1 + w * R2, R2)
            full_ref[mine, cols(b)] = a2[i, :, cols(b % 2)]
            for peer in peers:
                strip = full_ref.at[mine, cols(b)]
                send(strip, strip, (peer, z), f"g_second{b}")

    def back_second(b):
        arrived(r2.at[b], f"g_second{b}")
        peers, v, _, _ = first_peers(b)
        strip = full_ref.at[rows_of(c * R0 + v * R1, R1), cols(b)]
        for k, peer in enumerate(peers):
            send(strip, strip, (peer, z), f"g_first{b}_{k}")
        send(strip, strip, (partner, z), f"g_pair{b}_{n - 1}")

    def strip_of(core, b, k):
        _, v, _, _ = first_peers(b)
        place = plus(v, n - steps[k], n) if k < n - 1 else v
        return rows_of(core * R0 + place * R1, R1)

    def finish(core, b, k):
        strip = strip_of(core, b, k)
        gin_ref[strip, cols(b)] = full_ref[strip, cols(b)].astype(F32) * grad_scale

    def back_first(b, k):
        arrived(s1.at[b], f"g_first{b}_{k}")
        strip = full_ref.at[strip_of(c, b, k), cols(b)]
        send(strip, strip, (partner, z), f"g_pair{b}_{k}")

    def back_pair(b, k):
        arrived(s1.at[b], f"g_pair{b}_{k}")
        finish(1 - c, b, k)

    d_gated = mm(cot, wout_v[...], NT).astype(BF).astype(F32)
    g[4] = mm(gated, cot, TN).astype(BF)
    to_partner(4)
    normed_t = normed[...].T

    def weight_grad(b, d_proj):
        d = (d_proj.astype(BF).astype(F32) * dsil[:, cols(b)]).astype(BF)
        dpre[:, cols(b)] = d
        g[b] = mm(normed_t, d).astype(BF)
        to_partner(b)

    weight_grad(0, d_gated * nm)
    pair_sum(4)

    gn = d_gated * u32
    dm = inv_m * (
        gn - jnp.mean(gn, axis=1, keepdims=True) - nm * jnp.mean(gn * nm, axis=1, keepdims=True)
    )
    mixed[...] = dm
    d_v = []
    for i in range(HEADS // 2):
        dm_i = mixed[:, 128 * i : 128 * (i + 1)].astype(BF)
        part = None
        for j in range(2):
            term = mm(weights[2 * i + j], dm_i * side[j], TN)
            part = term if part is None else part + term
        d_v.append(part)
    weight_grad(1, jnp.concatenate(d_v, axis=1))
    pair_sum(0)

    d_q, d_k = [], []
    for i in range(HEADS // 2):
        q, k, v = pair(2, i), pair(3, i), pair(1, i)
        dm_i = mixed[:, 128 * i : 128 * (i + 1)].astype(BF)
        part_q = part_k = None
        for j in range(2):
            dw = mm(dm_i, v * side[j], NT).astype(BF).astype(F32)
            ds = (dw * dfac[2 * i + j]).astype(BF)
            term_q = mm(ds, k * side[j])
            term_k = mm(ds, q * side[j], TN)
            part_q = term_q if part_q is None else part_q + term_q
            part_k = term_k if part_k is None else part_k + term_k
        d_q.append(part_q)
        d_k.append(part_k)
        if i == 0:
            pair_sum(1)
    weight_grad(2, jnp.concatenate(d_q, axis=1))
    weight_grad(3, jnp.concatenate(d_k, axis=1))
    pair_sum(2)
    pair_sum(3)

    dn = mm(dpre[...], win_v[...], NT).astype(BF).astype(F32)
    first_sum(0)
    first_sum(1)
    nv = n32[...]
    de = cot.astype(F32) + inv_e * (
        dn - jnp.mean(dn, axis=1, keepdims=True) - nv * jnp.mean(dn * nv, axis=1, keepdims=True)
    )
    sg32 = mm(slot_hot, de.astype(BF))
    sg_s[...] = packed(sg32[:, :half], sg32[:, half:])
    sg_r[count - 1] = sg_s[t]

    RZ = R0 // nz
    CX = width // n
    arrived(ro1, "o_z")
    acc = h[4, rows_of(z * RZ, RZ)].astype(F32)
    for k in range(nz - 1):
        acc = acc + ro1[k].astype(F32)
    h[4, rows_of(z * RZ, RZ)] = acc.astype(BF)
    for k, (peer, place) in enumerate(zip(xs, plane(x, xs))):
        send(
            h.at[4, rows_of(z * RZ, RZ), rows_of(place * CX, CX)], ro2.at[k], (peer, z), "o_x"
        )
    second_sum(0)
    second_sum(1)
    first_sum(2)
    first_sum(3)
    arrived(ro2, "o_x")
    acc = h[4, rows_of(z * RZ, RZ), rows_of(x * CX, CX)].astype(F32)
    for k in range(n - 1):
        acc = acc + ro2[k].astype(F32)
    so2[...] = acc.astype(BF)
    ro3[y] = so2[...]
    for peer in ys:
        send(so2, ro3.at[y], (peer, z), "o_y")
    second_sum(2)
    second_sum(3)
    for k, peer in enumerate(ahead):
        send(sg_s.at[peer], sg_r.at[k], (peer, z), "slot")
    last_sum(0)

    arrived(ro3.at[pl.ds(0, n - 1)], "o_y")
    acc = ro3[0].astype(F32)
    for k in range(1, n):
        acc = acc + ro3[k].astype(F32)
    orows = rows_of(c * R0 + z * RZ, RZ)
    ocols = rows_of(x * CX, CX)
    fullo_ref[orows, ocols] = acc.astype(BF)
    for peer in xs:
        strip = fullo_ref.at[orows, ocols]
        send(strip, strip, (peer, z), "o_gx")

    last_sum(1)
    arrived(ro2, "o_gx")
    for peer in zs:
        strip = fullo_ref.at[orows]
        send(strip, strip, (t, peer), "o_gz")
    back_z(0)
    arrived(sg_r.at[pl.ds(0, count - 1)], "slot")
    tg_ref[...] = mm(row_hot[...], unpacked(sg_r), TN).astype(BF)
    back_z(1)
    back_second(0)
    back_second(1)
    back_second(2)
    back_second(3)
    for b in range(4):
        finish(c, b, n - 1)
    for k in reversed(range(n - 1)):
        back_first(0, k)
        back_first(1, k)
    arrived(ro1, "o_gz")
    strip = fullo_ref.at[own]
    send(strip, strip, (partner, z), "o_gp")
    for b in range(2):
        for k in range(n - 1):
            finish(c, b, k)
    gout_ref[own] = fullo_ref[own].astype(F32) * grad_scale
    for b in range(4):
        back_pair(b, n - 1)
    for k in reversed(range(n - 1)):
        back_pair(0, k)
        back_pair(1, k)
    for k in reversed(range(n - 1)):
        back_first(2, k)
        back_first(3, k)
        finish(c, 2, k)
        finish(c, 3, k)
    arrived(fullo_ref.at[other], "o_gp")
    gout_ref[other] = fullo_ref[other].astype(F32) * grad_scale
    for k in reversed(range(n - 1)):
        back_pair(2, k)
        back_pair(3, k)

    for ref, name in pending:
        pltpu.make_async_copy(ref, ref, send_sem.at[sem(name)]).wait()
    assert len(names) <= send_sem.shape[0]


def store(*refs):
    sems = refs[-1]
    copies = []
    for src, dst in zip(refs[:4], refs[4:8]):
        parts = 8 if src.dtype == F32 and src.shape[1] > src.shape[0] else 2
        size = src.shape[0] // parts
        for i in range(parts):
            part = pl.ds(i * size, size)
            copies.append(pltpu.make_async_copy(src.at[part], dst.at[part], sems.at[len(copies)]))
    for copy in copies:
        copy.start()
    for copy in copies:
        copy.wait()


def body(n, nz, table, fetch_rows, item_slot, seq_lengths, w_in, w_out, out_cot):
    _, count, cap = fetch_rows.shape
    rows, width = table.shape
    tokens = item_slot.shape[0]
    slots = count * cap
    half = width // 2
    R0 = width // 2
    R1 = R0 // n
    R2 = R1 // n
    CZ = 2 * width // nz
    any_ = pl.BlockSpec(memory_space=pl.ANY)
    vmem = pl.BlockSpec(memory_space=pltpu.VMEM)
    hbm = pl.BlockSpec(memory_space=pltpu.HBM)
    V = pltpu.VMEM
    grad_scale = float(tokens * count * nz) ** (-0.5)
    made = pl.pallas_call(
        functools.partial(kernel, n, nz, count, cap, rows, tokens, width, grad_scale),
        out_shape=(
            V((tokens, width), BF), V((rows, width), BF), V((width, 4 * width), F32), V((width, width), F32),
        ),
        in_specs=[hbm] * 7,
        out_specs=(vmem, vmem, vmem, vmem),
        scratch_shapes=[
            pltpu.SMEM((cap, count), jnp.int32), V((1, tokens), jnp.int32), pltpu.SMEM(seq_lengths.shape, jnp.int32),
            V((rows, width), BF), V((width, 4 * width), BF), V((width, width), BF), V((tokens, width), BF),
            V((count, 1, 128), jnp.int32), V((count, 1, 128), jnp.int32),
            V((count, 2 * cap, half), BF), V((count, 2 * cap, half), BF),
            V((count, 2 * cap, half), BF), V((count, 2 * cap, half), BF),
            V((slots, rows), BF), V((tokens, width), F32), V((tokens, width), F32), V((tokens, width), BF),
            V((tokens, 4 * width), BF), V((tokens, 4 * width), F32), V((tokens, 4 * width), BF),
            V((HEADS, tokens, tokens), BF), V((HEADS, tokens, tokens), F32),
            V((tokens, width), F32), V((tokens, tokens), F32),
            V((5, width, width), BF), V((5, R0, width), BF), V((5, R0, width), BF),
            V((4, n - 1, R1, width), BF), V((4, R1, width), BF),
            V((4, n - 1, R2, width), BF), V((2, R2, 2 * width), BF),
            V((2, nz - 1, R2, CZ), BF), V((2, R2, 2 * width), BF),
            V((nz - 1, R0 // nz, width), BF), V((n - 1, R0 // nz, width // n), BF),
            V((R0 // nz, width // n), BF), V((n, R0 // nz, width // n), BF),
            V((width, 4 * width), BF), V((width, width), BF),
            pltpu.SemaphoreType.DMA((7,)),
            pltpu.SemaphoreType.DMA((64,)),
            pltpu.SemaphoreType.DMA((64,)),
        ],
        compiler_params=pltpu.CompilerParams(
            collective_id=0, has_side_effects=True, vmem_limit_bytes=40 * 1024 * 1024
        ),
    )(
        *(
            pltpu.with_memory_space_constraint(v, pltpu.HBM)
            for v in (
                fetch_rows[0].T, item_slot.reshape(1, tokens), seq_lengths, table, w_in, w_out, out_cot
            )
        )
    )
    made = [pltpu.with_memory_space_constraint(v, pltpu.VMEM) for v in made]
    layer_out, table_grad, sum_in, sum_out = pl.pallas_call(
        store,
        out_shape=[jax.ShapeDtypeStruct(v.shape, v.dtype) for v in made],
        in_specs=[vmem] * 4,
        out_specs=[any_] * 4,
        scratch_shapes=[pltpu.SemaphoreType.DMA((16,))],
        compiler_params=pltpu.CompilerParams(vmem_limit_bytes=1024 * 1024),
    )(*made)
    return layer_out, table_grad[None], sum_in, sum_out


def solution(mesh):
    placed = (
        P("table", None),
        P(("table", "group"), None, None),
        P(("table", "group")),
        P(("table", "group"), None),
        P(),
        P(),
        P(("table", "group"), None),
    )
    n = math.isqrt(mesh.shape["table"] // 2)
    return jax.shard_map(
        functools.partial(body, n, mesh.shape["group"]),
        mesh=mesh,
        in_specs=placed,
        out_specs=(P(("table", "group"), None), P("group", "table", None), P(), P()),
        check_vma=False,
    )
```

```python
import functools
import math

import jax
import jax.numpy as jnp
from jax import lax
from jax.experimental import pallas as pl
from jax.experimental.pallas import tpu as pltpu
from jax.sharding import PartitionSpec as P

HEADS = 8
EPS = 1e-05
MESH = pl.DeviceIdType.MESH
BF = jnp.bfloat16
F32 = jnp.float32

NN = (((1,), (0,)), ((), ()))
NT = (((1,), (1,)), ((), ()))
TN = (((0,), (0,)), ((), ()))


def mm(a, b, dims=NN):
    return lax.dot_general(a, b, dims, preferred_element_type=F32)


def rows_of(start, size):
    return pl.ds(pl.multiple_of(start, size), size)


def kernel(
    n, nz, count, cap, rows, tokens, width, grad_scale,
    fetch_hbm, slot_hbm, len_hbm, table_hbm, win_hbm, wout_hbm, cot_hbm,
    out_ref, tg_ref, gin_ref, gout_ref,
    fetch_ref, slot_ref, len_ref, table_v, win_v, wout_v, cot_v,
    req_s, req_r, found, rows_r, sg_s, sg_r,
    row_hot, tok_hot, dg, gated_v, emb, n32, normed, proj, dsil, dpre, weights, dfac, mixed, allowed,
    g, pr, h, r1, s1, r2, s2, r3, a2,
    ro1, ro2, so2, ro3, full_ref, fullo_ref,
    load_sem, send_sem, recv_sem,
):
    t = lax.axis_index("table")
    z = lax.axis_index("group")
    x = lax.div(t, 2 * n)
    y = lax.rem(lax.div(t, 2), n)
    c = lax.rem(t, 2)
    slots = count * cap
    half = width // 2
    R0 = width // 2
    R1 = R0 // n
    R2 = R1 // n
    CZ = 2 * width // nz

    def at(px, py, pc):
        return (px * n + py) * 2 + pc

    def plus(v, d, m):
        return lax.rem(v + d, m)

    def far(d, m):
        return min(d, m - d)

    offsets = [(dx, dy, dc) for dx in range(n) for dy in range(n) for dc in range(2)][1:]
    offsets.sort(key=lambda o: (-far(o[0], n) - far(o[1], n), o))
    steps = sorted(range(1, n), key=lambda d: -far(d, n))
    zsteps = sorted(range(1, nz), key=lambda d: -far(d, nz))
    ahead = [at(plus(x, dx, n), plus(y, dy, n), plus(c, dc, 2)) for dx, dy, dc in offsets]
    behind = [at(plus(x, n - dx, n), plus(y, n - dy, n), plus(c, 2 - dc, 2)) for dx, dy, dc in offsets]
    zs = [plus(z, d, nz) for d in zsteps]
    xs = [at(plus(x, d, n), y, c) for d in steps]
    ys = [at(x, plus(y, d, n), c) for d in steps]
    partner = at(x, y, 1 - c)

    loads = [
        pltpu.make_async_copy(src, dst, load_sem.at[i])
        for i, (src, dst) in enumerate(
            (
                (fetch_hbm, fetch_ref), (len_hbm, len_ref), (slot_hbm, slot_ref),
                (table_hbm, table_v), (win_hbm, win_v), (wout_hbm, wout_v), (cot_hbm, cot_v),
            )
        )
    ]
    loads[0].start()
    barrier = pltpu.get_barrier_semaphore()
    for peer in ahead:
        pl.semaphore_signal(barrier, inc=1, device_id=(peer, z), device_id_type=MESH)
    for peer in zs:
        pl.semaphore_signal(barrier, inc=1, device_id=(t, peer), device_id_type=MESH)
    for copy in loads[1:]:
        copy.start()

    names = {}
    pending = []

    def sem(name):
        return names.setdefault(name, len(names))

    def send(src, dst, to, name):
        i = sem(name)
        pltpu.make_async_remote_copy(
            src_ref=src, dst_ref=dst, send_sem=send_sem.at[i], recv_sem=recv_sem.at[i],
            device_id=to, device_id_type=MESH,
        ).start()

    def arrived(ref, name):
        pltpu.make_async_copy(ref, ref, recv_sem.at[sem(name)]).wait()
        pending.append((ref, name))

    loads[0].wait()
    lane = lax.broadcasted_iota(jnp.int32, (1, 128), 1)
    for o in range(count):
        line = jnp.zeros((1, 128), jnp.int32)
        for e in range(cap):
            line = jnp.where(lane == e, fetch_ref[e, o], line)
        req_s[o] = line
    pl.semaphore_wait(barrier, count - 1 + nz - 1)
    for k, peer in enumerate(ahead):
        send(req_s.at[peer], req_r.at[k], (peer, z), f"list{0 if k < count // 2 else count // 2}")
    req_r[count - 1] = req_s[t]

    loads[1].wait()
    loads[2].wait()
    ends = []
    total = jnp.int32(0)
    for s in range(len_ref.shape[1]):
        total = total + len_ref[0, s]
        ends.append(total)
    pos_i = lax.broadcasted_iota(jnp.int32, (tokens, tokens), 0)
    pos_j = lax.broadcasted_iota(jnp.int32, (tokens, tokens), 1)
    first = jnp.zeros((tokens, tokens), jnp.int32)
    for e in ends:
        first = jnp.where(pos_i >= e, e, first)
    allowed[...] = jnp.where((pos_j >= first) & (pos_j <= pos_i), 1.0, 0.0).astype(BF)
    slot_hot = jnp.where(
        lax.broadcasted_iota(jnp.int32, (slots, tokens), 0) == slot_ref[...], 1.0, 0.0
    ).astype(BF)

    def hot_rows(start, size):
        lists = jnp.broadcast_to(req_r[start : start + size].astype(F32), (size, cap, 128))
        diagonal = lax.broadcasted_iota(jnp.int32, (size, cap, 128), 1) == lax.broadcasted_iota(
            jnp.int32, (size, cap, 128), 2
        )
        wanted = jnp.sum(jnp.where(diagonal, lists, 0.0), axis=2, keepdims=True).reshape(size * cap, 1)
        lane = lax.broadcasted_iota(jnp.int32, (size * cap, 128), 1).astype(F32)
        row_hot[start * cap : (start + size) * cap] = jnp.concatenate(
            [jnp.where(wanted == lane + 128.0 * i, 1.0, 0.0).astype(BF) for i in range(rows // 128)], axis=1
        )

    def packed(lo, hi):
        return jnp.concatenate([lo.reshape(-1, cap, half), hi.reshape(-1, cap, half)], axis=1).astype(BF)

    def unpacked(ref):
        v = ref[...].astype(F32)
        return jnp.concatenate(
            [v[:, :cap].reshape(slots, half), v[:, cap:].reshape(slots, half)], axis=1
        ).astype(BF)

    cut = count // 2
    for start, size, got in ((cut, cut, cut - 1), (0, cut, cut)):
        arrived(req_r.at[pl.ds(start, got)], f"list{start}")
        if start:
            loads[3].wait()
        hot_rows(start, size)
        hot = row_hot[start * cap : (start + size) * cap]
        found[start : start + size] = packed(mm(hot, table_v[:, :half]), mm(hot, table_v[:, half:]))
        for k in range(start, start + got):
            send(found.at[k], rows_r.at[t], (behind[k], z), "rows")
    rows_r[t] = found[count - 1]
    tok_hot[...] = slot_hot.T
    for i in (4, 5, 6):
        loads[i].wait()
    cot = cot_v[...]
    dg[...] = mm(cot, wout_v[...], NT).astype(BF).astype(F32)
    arrived(rows_r.at[pl.ds(0, count - 1)], "rows")

    e32 = mm(tok_hot[...], unpacked(rows_r))
    emb[...] = e32
    cen = e32 - jnp.mean(e32, axis=1, keepdims=True)
    inv_e = lax.rsqrt(jnp.mean(cen * cen, axis=1, keepdims=True) + EPS)
    n32[...] = cen * inv_e
    normed[...] = n32[...].astype(BF)

    def cols(b):
        return slice(b * width, (b + 1) * width)

    for b in range(4):
        p = mm(normed[...], win_v[:, cols(b)])
        sg = 0.5 + 0.5 * jnp.tanh(0.5 * p)
        act = p * sg
        proj[:, cols(b)] = act.astype(BF)
        dsil[:, cols(b)] = (sg + act * (1.0 - sg)).astype(BF)

    lanes = lax.broadcasted_iota(jnp.int32, (1, 128), 1)
    side = [
        jnp.where(lanes < 64, 1.0, 0.0).astype(BF),
        jnp.where(lanes >= 64, 1.0, 0.0).astype(BF),
    ]

    def pair(b, i):
        return proj[:, b * width + 128 * i : b * width + 128 * (i + 1)]

    scale = (width // HEADS) ** -0.5
    mid = tokens // 2

    def lower(f, *arrays):
        top = f(*(v[:mid, :mid] for v in arrays))
        low = f(*(v[mid:] for v in arrays))
        none = jnp.zeros((mid, tokens - mid), BF)
        return [
            jnp.concatenate([jnp.concatenate([a, none], axis=1), b], axis=0) for a, b in zip(top, low)
        ]

    def score(s, keep):
        sg = 0.5 + 0.5 * jnp.tanh((0.5 * scale) * s)
        act = (scale * s) * sg
        return act.astype(BF) * keep, (sg + act * (1.0 - sg)).astype(BF) * (keep * BF(scale))

    for i in range(HEADS // 2):
        q, k, v = pair(2, i), pair(3, i), pair(1, i)
        part = None
        for j in range(2):
            w, factor = lower(score, mm(q, k * side[j], NT), allowed[...])
            weights[2 * i + j] = w
            dfac[2 * i + j] = factor
            term = mm(w, v * side[j])
            part = term if part is None else part + term
        mixed[:, 128 * i : 128 * (i + 1)] = part

    m32 = mixed[...]
    cen = m32 - jnp.mean(m32, axis=1, keepdims=True)
    inv_m = lax.rsqrt(jnp.mean(cen * cen, axis=1, keepdims=True) + EPS)
    nm = cen * inv_m
    u32 = proj[:, cols(0)].astype(F32)
    gated = (nm * u32).astype(BF)
    gated_v[...] = gated

    own = rows_of(c * R0, R0)
    other = rows_of((1 - c) * R0, R0)

    def to_partner(b):
        send(g.at[b, other], pr.at[b], (partner, z), f"pair{b}")

    def first_peers(b):
        return (xs, x, ys, y) if b % 2 == 0 else (ys, y, xs, x)

    def plane(v):
        return [plus(v, d, n) for d in steps]

    def pair_sum(b):
        arrived(pr.at[b], f"pair{b}")
        h[b] = (g[b, own].astype(F32) + pr[b].astype(F32)).astype(BF)
        if b < 4:
            peers, v, _, w = first_peers(b)
            for j, sub in enumerate(plane(w) + [w]):
                for k, (peer, place) in enumerate(zip(peers, plane(v))):
                    send(h.at[b, rows_of(place * R1 + sub * R2, R2)], r1.at[b, j, k], (peer, z), f"first{b}_{j}")
        else:
            for k, place in enumerate(zs):
                send(h.at[b, rows_of(place * (R0 // nz), R0 // nz)], ro1.at[k], (t, place), "o_z")

    def first_sum(b):
        _, v, peers, w = first_peers(b)
        for j, sub in enumerate(plane(w) + [w]):
            arrived(r1.at[b, j], f"first{b}_{j}")
            acc = h[b, rows_of(v * R1 + sub * R2, R2)].astype(F32)
            for k in range(n - 1):
                acc = acc + r1[b, j, k].astype(F32)
            s1[b, j] = acc.astype(BF)
            if j < n - 1:
                send(s1.at[b, j], r2.at[b, j], (peers[j], z), f"second{b}")

    def second_sum(b):
        arrived(r2.at[b], f"second{b}")
        acc = s1[b, n - 1].astype(F32)
        for k in range(n - 1):
            acc = acc + r2[b, k].astype(F32)
        s2[b // 2, :, cols(b % 2)] = acc.astype(BF)
        if b % 2 == 1:
            for k, place in enumerate(zs):
                send(
                    s2.at[b // 2, :, rows_of(place * CZ, CZ)], r3.at[b // 2, k], (t, place), f"last{b // 2}"
                )

    zcols = rows_of(z * CZ, CZ)

    def last_sum(i):
        arrived(r3.at[i], f"last{i}")
        acc = s2[i, :, zcols].astype(F32)
        for k in range(nz - 1):
            acc = acc + r3[i, k].astype(F32)
        a2[i, :, zcols] = acc.astype(BF)
        for peer in zs:
            send(a2.at[i, :, zcols], a2.at[i, :, zcols], (t, peer), f"g_z{i}")

    def back_z(i):
        arrived(a2.at[i, :, pl.ds(0, CZ * (nz - 1))], f"g_z{i}")
        for b in (2 * i, 2 * i + 1):
            _, v, peers, w = first_peers(b)
            mine = rows_of(c * R0 + v * R1 + w * R2, R2)
            full_ref[mine, cols(b)] = a2[i, :, cols(b % 2)]
            strip = full_ref.at[mine, cols(b)]
            for k, peer in enumerate(peers):
                send(strip, strip, (peer, z), f"g_second{b}_{k}")
        for b in (2 * i, 2 * i + 1):
            pass_on(b, n - 1)

    def pass_on(b, k):
        peers, v, _, w = first_peers(b)
        place = plus(w, n - steps[k], n) if k < n - 1 else w
        strip = full_ref.at[rows_of(c * R0 + v * R1 + place * R2, R2), cols(b)]
        for i, peer in enumerate(peers):
            send(strip, strip, (peer, z), f"g_first{b}_{i}")

    def back_second(b, k):
        arrived(s1.at[b, 0], f"g_second{b}_{k}")
        pass_on(b, k)

    def own_strip(b):
        strip = full_ref.at[strip_of(c, b, n - 1), cols(b)]
        send(strip, strip, (partner, z), f"g_pair{b}_{n - 1}")

    def strip_of(core, b, k):
        _, v, _, _ = first_peers(b)
        place = plus(v, n - steps[k], n) if k < n - 1 else v
        return rows_of(core * R0 + place * R1, R1)

    def finish(core, b, k):
        strip = strip_of(core, b, k)
        gin_ref[strip, cols(b)] = full_ref[strip, cols(b)].astype(F32) * grad_scale

    def back_first(b, k):
        arrived(s1.at[b], f"g_first{b}_{k}")
        strip = full_ref.at[strip_of(c, b, k), cols(b)]
        send(strip, strip, (partner, z), f"g_pair{b}_{k}")

    def back_pair(b, k):
        arrived(s1.at[b], f"g_pair{b}_{k}")
        finish(1 - c, b, k)

    d_gated = dg[...]
    g[4] = mm(gated, cot, TN).astype(BF)
    to_partner(4)
    normed_t = normed[...].T

    def weight_grad(b, d_proj):
        d = d_proj.astype(BF) * dsil[:, cols(b)]
        dpre[:, cols(b)] = d
        g[b] = mm(normed_t, d).astype(BF)
        to_partner(b)

    weight_grad(0, d_gated * nm)

    gn = d_gated * u32
    dm = inv_m * (
        gn - jnp.mean(gn, axis=1, keepdims=True) - nm * jnp.mean(gn * nm, axis=1, keepdims=True)
    )
    mixed[...] = dm
    d_v = []
    for i in range(HEADS // 2):
        dm_i = mixed[:, 128 * i : 128 * (i + 1)].astype(BF)
        part = None
        for j in range(2):
            term = mm(weights[2 * i + j], dm_i * side[j], TN)
            part = term if part is None else part + term
        d_v.append(part)
    pair_sum(4)
    weight_grad(1, jnp.concatenate(d_v, axis=1))

    d_q, d_k = [], []
    for i in range(HEADS // 2):
        q, k, v = pair(2, i), pair(3, i), pair(1, i)
        dm_i = mixed[:, 128 * i : 128 * (i + 1)].astype(BF)
        part_q = part_k = None
        for j in range(2):
            (ds,) = lower(
                lambda dw, factor: (dw.astype(BF) * factor,), mm(dm_i, v * side[j], NT), dfac[2 * i + j]
            )
            term_q = mm(ds, k * side[j])
            term_k = mm(ds, q * side[j], TN)
            part_q = term_q if part_q is None else part_q + term_q
            part_k = term_k if part_k is None else part_k + term_k
        d_q.append(part_q)
        d_k.append(part_k)
        if i == 0:
            pair_sum(0)
        if i == 2:
            pair_sum(1)
    weight_grad(2, jnp.concatenate(d_q, axis=1))
    weight_grad(3, jnp.concatenate(d_k, axis=1))
    pair_sum(2)
    pair_sum(3)

    out_ref[...] = (emb[...] + mm(gated_v[...], wout_v[...])).astype(BF)
    dn = mm(dpre[...], win_v[...], NT).astype(BF).astype(F32)
    first_sum(0)
    first_sum(1)
    nv = n32[...]
    de = cot.astype(F32) + inv_e * (
        dn - jnp.mean(dn, axis=1, keepdims=True) - nv * jnp.mean(dn * nv, axis=1, keepdims=True)
    )
    sg32 = mm(slot_hot, de.astype(BF))
    sg_s[...] = packed(sg32[:, :half], sg32[:, half:])
    sg_r[count - 1] = sg_s[t]

    RZ = R0 // nz
    CX = width // n
    arrived(ro1, "o_z")
    acc = h[4, rows_of(z * RZ, RZ)].astype(F32)
    for k in range(nz - 1):
        acc = acc + ro1[k].astype(F32)
    h[4, rows_of(z * RZ, RZ)] = acc.astype(BF)
    for k, (peer, place) in enumerate(zip(xs, plane(x))):
        send(
            h.at[4, rows_of(z * RZ, RZ), rows_of(place * CX, CX)], ro2.at[k], (peer, z), "o_x"
        )
    second_sum(0)
    second_sum(1)
    first_sum(2)
    first_sum(3)
    arrived(ro2, "o_x")
    acc = h[4, rows_of(z * RZ, RZ), rows_of(x * CX, CX)].astype(F32)
    for k in range(n - 1):
        acc = acc + ro2[k].astype(F32)
    so2[...] = acc.astype(BF)
    ro3[y] = so2[...]
    for peer in ys:
        send(so2, ro3.at[y], (peer, z), "o_y")
    second_sum(2)
    second_sum(3)
    for k, peer in enumerate(ahead):
        send(sg_s.at[peer], sg_r.at[k], (peer, z), "slot")
    last_sum(0)

    arrived(ro3.at[pl.ds(0, n - 1)], "o_y")
    acc = ro3[0].astype(F32)
    for k in range(1, n):
        acc = acc + ro3[k].astype(F32)
    orows = rows_of(c * R0 + z * RZ, RZ)
    ocols = rows_of(x * CX, CX)
    fullo_ref[orows, ocols] = acc.astype(BF)
    for peer in xs:
        strip = fullo_ref.at[orows, ocols]
        send(strip, strip, (peer, z), "o_gx")

    last_sum(1)
    arrived(ro2, "o_gx")
    for peer in zs:
        strip = fullo_ref.at[orows]
        send(strip, strip, (t, peer), "o_gz")
    back_z(0)
    back_z(1)
    arrived(sg_r.at[pl.ds(0, count - 1)], "slot")
    tg_ref[...] = mm(row_hot[...], unpacked(sg_r), TN).astype(BF)
    for i in (0, 2):
        for k in reversed(range(n - 1)):
            back_second(i, k)
            back_second(i + 1, k)
        own_strip(i)
        own_strip(i + 1)
    for b in range(4):
        finish(c, b, n - 1)
    for k in reversed(range(n - 1)):
        back_first(0, k)
        back_first(1, k)
    arrived(ro1, "o_gz")
    strip = fullo_ref.at[own]
    send(strip, strip, (partner, z), "o_gp")
    for b in range(2):
        for k in range(n - 1):
            finish(c, b, k)
    gout_ref[own] = fullo_ref[own].astype(F32) * grad_scale
    for b in range(4):
        back_pair(b, n - 1)
    for k in reversed(range(n - 1)):
        back_pair(0, k)
        back_pair(1, k)
    for k in reversed(range(n - 1)):
        back_first(2, k)
        back_first(3, k)
        finish(c, 2, k)
        finish(c, 3, k)
    arrived(fullo_ref.at[other], "o_gp")
    gout_ref[other] = fullo_ref[other].astype(F32) * grad_scale
    for k in reversed(range(n - 1)):
        back_pair(2, k)
        back_pair(3, k)

    for ref, name in pending:
        pltpu.make_async_copy(ref, ref, send_sem.at[sem(name)]).wait()
    assert len(names) <= send_sem.shape[0]


def store(*refs):
    sems = refs[-1]
    copies = []
    for src, dst in zip(refs[:4], refs[4:8]):
        parts = 8 if src.dtype == F32 and src.shape[1] > src.shape[0] else 2
        size = src.shape[0] // parts
        for i in range(parts):
            part = pl.ds(i * size, size)
            copies.append(pltpu.make_async_copy(src.at[part], dst.at[part], sems.at[len(copies)]))
    for copy in copies:
        copy.start()
    for copy in copies:
        copy.wait()


def body(n, nz, table, fetch_rows, item_slot, seq_lengths, w_in, w_out, out_cot):
    _, count, cap = fetch_rows.shape
    rows, width = table.shape
    tokens = item_slot.shape[0]
    slots = count * cap
    half = width // 2
    R0 = width // 2
    R1 = R0 // n
    R2 = R1 // n
    CZ = 2 * width // nz
    any_ = pl.BlockSpec(memory_space=pl.ANY)
    vmem = pl.BlockSpec(memory_space=pltpu.VMEM)
    hbm = pl.BlockSpec(memory_space=pltpu.HBM)
    V = pltpu.VMEM
    grad_scale = float(tokens * count * nz) ** (-0.5)
    made = pl.pallas_call(
        functools.partial(kernel, n, nz, count, cap, rows, tokens, width, grad_scale),
        out_shape=(
            V((tokens, width), BF), V((rows, width), BF), V((width, 4 * width), F32), V((width, width), F32),
        ),
        in_specs=[hbm] * 7,
        out_specs=(vmem, vmem, vmem, vmem),
        scratch_shapes=[
            pltpu.SMEM((cap, count), jnp.int32), V((1, tokens), jnp.int32), pltpu.SMEM(seq_lengths.shape, jnp.int32),
            V((rows, width), BF), V((width, 4 * width), BF), V((width, width), BF), V((tokens, width), BF),
            V((count, 1, 128), jnp.int32), V((count, 1, 128), jnp.int32),
            V((count, 2 * cap, half), BF), V((count, 2 * cap, half), BF),
            V((count, 2 * cap, half), BF), V((count, 2 * cap, half), BF),
            V((slots, rows), BF), V((tokens, slots), BF), V((tokens, width), F32), V((tokens, width), BF), V((tokens, width), F32), V((tokens, width), F32), V((tokens, width), BF),
            V((tokens, 4 * width), BF), V((tokens, 4 * width), BF), V((tokens, 4 * width), BF),
            V((HEADS, tokens, tokens), BF), V((HEADS, tokens, tokens), BF),
            V((tokens, width), F32), V((tokens, tokens), BF),
            V((5, width, width), BF), V((5, R0, width), BF), V((5, R0, width), BF),
            V((4, n, n - 1, R2, width), BF), V((4, n, R2, width), BF),
            V((4, n - 1, R2, width), BF), V((2, R2, 2 * width), BF),
            V((2, nz - 1, R2, CZ), BF), V((2, R2, 2 * width), BF),
            V((nz - 1, R0 // nz, width), BF), V((n - 1, R0 // nz, width // n), BF),
            V((R0 // nz, width // n), BF), V((n, R0 // nz, width // n), BF),
            V((width, 4 * width), BF), V((width, width), BF),
            pltpu.SemaphoreType.DMA((7,)),
            pltpu.SemaphoreType.DMA((96,)),
            pltpu.SemaphoreType.DMA((96,)),
        ],
        compiler_params=pltpu.CompilerParams(
            collective_id=0, has_side_effects=True, vmem_limit_bytes=40 * 1024 * 1024
        ),
    )(
        *(
            pltpu.with_memory_space_constraint(v, pltpu.HBM)
            for v in (
                fetch_rows[0].T, item_slot.reshape(1, tokens), seq_lengths, table, w_in, w_out, out_cot
            )
        )
    )
    made = [pltpu.with_memory_space_constraint(v, pltpu.VMEM) for v in made]
    layer_out, table_grad, sum_in, sum_out = pl.pallas_call(
        store,
        out_shape=[jax.ShapeDtypeStruct(v.shape, v.dtype) for v in made],
        in_specs=[vmem] * 4,
        out_specs=[any_] * 4,
        scratch_shapes=[pltpu.SemaphoreType.DMA((16,))],
        compiler_params=pltpu.CompilerParams(vmem_limit_bytes=1024 * 1024),
    )(*made)
    return layer_out, table_grad[None], sum_in, sum_out


def solution(mesh):
    placed = (
        P("table", None),
        P(("table", "group"), None, None),
        P(("table", "group")),
        P(("table", "group"), None),
        P(),
        P(),
        P(("table", "group"), None),
    )
    n = math.isqrt(mesh.shape["table"] // 2)
    return jax.shard_map(
        functools.partial(body, n, mesh.shape["group"]),
        mesh=mesh,
        in_specs=placed,
        out_specs=(P(("table", "group"), None), P("group", "table", None), P(), P()),
        check_vma=False,
    )
```

```python
import functools
import math

import jax
import jax.numpy as jnp
from jax import lax
from jax.experimental import pallas as pl
from jax.experimental.pallas import tpu as pltpu
from jax.sharding import PartitionSpec as P

HEADS = 8
EPS = 1e-05
MESH = pl.DeviceIdType.MESH
BF = jnp.bfloat16
F32 = jnp.float32

NN = (((1,), (0,)), ((), ()))
NT = (((1,), (1,)), ((), ()))
TN = (((0,), (0,)), ((), ()))


def mm(a, b, dims=NN):
    return lax.dot_general(a, b, dims, preferred_element_type=F32)


def rows_of(start, size):
    return pl.ds(pl.multiple_of(start, size), size)


def kernel(
    n, nz, count, cap, rows, tokens, width, grad_scale,
    fetch_hbm, slot_hbm, len_hbm, table_hbm, win_hbm, wout_hbm, cot_hbm,
    out_ref, tg_ref, gin_ref, gout_ref,
    fetch_ref, slot_ref, len_ref, table_v, win_v, wout_v, cot_v,
    req_s, req_r, found, rows_r, sg_s, sg_r,
    row_hot, tok_hot, dg, gated_v, emb, n32, normed, proj, dsil, dpre, weights, dfac, mixed, allowed,
    g, pr, h, r1, s1, r2, s2, r3, a2,
    ro1, ro2, so2, ro3, full_ref, fullo_ref,
    load_sem, send_sem, recv_sem,
):
    t = lax.axis_index("table")
    z = lax.axis_index("group")
    x = lax.div(t, 2 * n)
    y = lax.rem(lax.div(t, 2), n)
    c = lax.rem(t, 2)
    slots = count * cap
    half = width // 2
    R0 = width // 2
    R1 = R0 // n
    R2 = R1 // n
    CZ = 2 * width // nz

    def at(px, py, pc):
        return (px * n + py) * 2 + pc

    def plus(v, d, m):
        return lax.rem(v + d, m)

    def far(d, m):
        return min(d, m - d)

    offsets = [(dx, dy, dc) for dx in range(n) for dy in range(n) for dc in range(2)][1:]
    offsets.sort(key=lambda o: (-far(o[0], n) - far(o[1], n), o))
    steps = sorted(range(1, n), key=lambda d: -far(d, n))
    zsteps = sorted(range(1, nz), key=lambda d: -far(d, nz))
    ahead = [at(plus(x, dx, n), plus(y, dy, n), plus(c, dc, 2)) for dx, dy, dc in offsets]
    behind = [at(plus(x, n - dx, n), plus(y, n - dy, n), plus(c, 2 - dc, 2)) for dx, dy, dc in offsets]
    zs = [plus(z, d, nz) for d in zsteps]
    xs = [at(plus(x, d, n), y, c) for d in steps]
    ys = [at(x, plus(y, d, n), c) for d in steps]
    partner = at(x, y, 1 - c)

    loads = [
        pltpu.make_async_copy(src, dst, load_sem.at[i])
        for i, (src, dst) in enumerate(
            (
                (fetch_hbm, fetch_ref), (len_hbm, len_ref), (slot_hbm, slot_ref),
                (table_hbm, table_v), (win_hbm, win_v), (wout_hbm, wout_v), (cot_hbm, cot_v),
            )
        )
    ]
    loads[0].start()
    barrier = pltpu.get_barrier_semaphore()
    for peer in ahead:
        pl.semaphore_signal(barrier, inc=1, device_id=(peer, z), device_id_type=MESH)
    for peer in zs:
        pl.semaphore_signal(barrier, inc=1, device_id=(t, peer), device_id_type=MESH)
    for copy in loads[1:]:
        copy.start()

    names = {}
    pending = []

    def sem(name):
        return names.setdefault(name, len(names))

    def send(src, dst, to, name):
        i = sem(name)
        pltpu.make_async_remote_copy(
            src_ref=src, dst_ref=dst, send_sem=send_sem.at[i], recv_sem=recv_sem.at[i],
            device_id=to, device_id_type=MESH,
        ).start()

    def arrived(ref, name):
        pltpu.make_async_copy(ref, ref, recv_sem.at[sem(name)]).wait()
        pending.append((ref, name))

    loads[0].wait()
    lane = lax.broadcasted_iota(jnp.int32, (1, 128), 1)
    for o in range(count):
        line = jnp.zeros((1, 128), jnp.int32)
        for e in range(cap):
            line = jnp.where(lane == e, fetch_ref[e, o], line)
        req_s[o] = line
    pl.semaphore_wait(barrier, count - 1 + nz - 1)
    for k, peer in enumerate(ahead):
        send(req_s.at[peer], req_r.at[k], (peer, z), f"list{0 if k < count // 2 else count // 2}")
    req_r[count - 1] = req_s[t]

    loads[1].wait()
    loads[2].wait()
    ends = []
    total = jnp.int32(0)
    for s in range(len_ref.shape[1]):
        total = total + len_ref[0, s]
        ends.append(total)
    pos_i = lax.broadcasted_iota(jnp.int32, (tokens, tokens), 0)
    pos_j = lax.broadcasted_iota(jnp.int32, (tokens, tokens), 1)
    first = jnp.zeros((tokens, tokens), jnp.int32)
    for e in ends:
        first = jnp.where(pos_i >= e, e, first)
    allowed[...] = jnp.where((pos_j >= first) & (pos_j <= pos_i), 1.0, 0.0).astype(BF)
    slot_hot = jnp.where(
        lax.broadcasted_iota(jnp.int32, (slots, tokens), 0) == slot_ref[...], 1.0, 0.0
    ).astype(BF)

    def hot_rows(start, size):
        lists = jnp.broadcast_to(req_r[start : start + size].astype(F32), (size, cap, 128))
        diagonal = lax.broadcasted_iota(jnp.int32, (size, cap, 128), 1) == lax.broadcasted_iota(
            jnp.int32, (size, cap, 128), 2
        )
        wanted = jnp.sum(jnp.where(diagonal, lists, 0.0), axis=2, keepdims=True).reshape(size * cap, 1)
        lane = lax.broadcasted_iota(jnp.int32, (size * cap, 128), 1).astype(F32)
        row_hot[start * cap : (start + size) * cap] = jnp.concatenate(
            [jnp.where(wanted == lane + 128.0 * i, 1.0, 0.0).astype(BF) for i in range(rows // 128)], axis=1
        )

    def packed(lo, hi):
        return jnp.concatenate([lo.reshape(-1, cap, half), hi.reshape(-1, cap, half)], axis=1).astype(BF)

    def unpacked(ref):
        v = ref[...].astype(F32)
        return jnp.concatenate(
            [v[:, :cap].reshape(slots, half), v[:, cap:].reshape(slots, half)], axis=1
        ).astype(BF)

    cut = count // 2
    for start, size, got in ((cut, cut, cut - 1), (0, cut, cut)):
        arrived(req_r.at[pl.ds(start, got)], f"list{start}")
        if start:
            loads[3].wait()
        hot_rows(start, size)
        hot = row_hot[start * cap : (start + size) * cap]
        found[start : start + size] = packed(mm(hot, table_v[:, :half]), mm(hot, table_v[:, half:]))
        for k in range(start, start + got):
            send(found.at[k], rows_r.at[t], (behind[k], z), "rows")
    rows_r[t] = found[count - 1]
    tok_hot[...] = slot_hot.T
    for i in (4, 5, 6):
        loads[i].wait()
    cot = cot_v[...]
    dg[...] = mm(cot, wout_v[...], NT).astype(BF).astype(F32)
    arrived(rows_r.at[pl.ds(0, count - 1)], "rows")

    e32 = mm(tok_hot[...], unpacked(rows_r))
    emb[...] = e32
    cen = e32 - jnp.mean(e32, axis=1, keepdims=True)
    inv_e = lax.rsqrt(jnp.mean(cen * cen, axis=1, keepdims=True) + EPS)
    n32[...] = cen * inv_e
    normed[...] = n32[...].astype(BF)

    def cols(b):
        return slice(b * width, (b + 1) * width)

    for b in range(4):
        p = mm(normed[...], win_v[:, cols(b)])
        sg = 0.5 + 0.5 * jnp.tanh(0.5 * p)
        act = p * sg
        proj[:, cols(b)] = act.astype(BF)
        dsil[:, cols(b)] = (sg + act * (1.0 - sg)).astype(BF)

    lanes = lax.broadcasted_iota(jnp.int32, (1, 128), 1)
    side = [
        jnp.where(lanes < 64, 1.0, 0.0).astype(BF),
        jnp.where(lanes >= 64, 1.0, 0.0).astype(BF),
    ]

    def pair(b, i):
        return proj[:, b * width + 128 * i : b * width + 128 * (i + 1)]

    scale = (width // HEADS) ** -0.5
    mid = tokens // 2

    def lower(f, *arrays):
        top = f(*(v[:mid, :mid] for v in arrays))
        low = f(*(v[mid:] for v in arrays))
        none = jnp.zeros((mid, tokens - mid), BF)
        return [
            jnp.concatenate([jnp.concatenate([a, none], axis=1), b], axis=0) for a, b in zip(top, low)
        ]

    def score(s, keep):
        sg = 0.5 + 0.5 * jnp.tanh((0.5 * scale) * s)
        act = (scale * s) * sg
        return act.astype(BF) * keep, (sg + act * (1.0 - sg)).astype(BF) * (keep * BF(scale))

    for i in range(HEADS // 2):
        q, k, v = pair(2, i), pair(3, i), pair(1, i)
        part = None
        for j in range(2):
            w, factor = lower(score, mm(q, k * side[j], NT), allowed[...])
            weights[2 * i + j] = w
            dfac[2 * i + j] = factor
            term = mm(w, v * side[j])
            part = term if part is None else part + term
        mixed[:, 128 * i : 128 * (i + 1)] = part

    m32 = mixed[...]
    cen = m32 - jnp.mean(m32, axis=1, keepdims=True)
    inv_m = lax.rsqrt(jnp.mean(cen * cen, axis=1, keepdims=True) + EPS)
    nm = cen * inv_m
    u32 = proj[:, cols(0)].astype(F32)
    gated = (nm * u32).astype(BF)
    gated_v[...] = gated

    own = rows_of(c * R0, R0)
    other = rows_of((1 - c) * R0, R0)

    def to_partner(b):
        send(g.at[b, other], pr.at[b], (partner, z), f"pair{b}")

    def first_peers(b):
        return (xs, x, ys, y) if b % 2 == 0 else (ys, y, xs, x)

    def plane(v):
        return [plus(v, d, n) for d in steps]

    def pair_sum(b):
        arrived(pr.at[b], f"pair{b}")
        h[b] = (g[b, own].astype(F32) + pr[b].astype(F32)).astype(BF)
        if b < 4:
            peers, v, _, w = first_peers(b)
            for j, sub in enumerate(plane(w) + [w]):
                for k, (peer, place) in enumerate(zip(peers, plane(v))):
                    send(h.at[b, rows_of(place * R1 + sub * R2, R2)], r1.at[b, j, k], (peer, z), f"first{b}_{j}")
        else:
            for k, place in enumerate(zs):
                send(h.at[b, rows_of(place * (R0 // nz), R0 // nz)], ro1.at[k], (t, place), "o_z")

    def first_sum(b):
        _, v, peers, w = first_peers(b)
        for j, sub in enumerate(plane(w) + [w]):
            arrived(r1.at[b, j], f"first{b}_{j}")
            acc = h[b, rows_of(v * R1 + sub * R2, R2)].astype(F32)
            for k in range(n - 1):
                acc = acc + r1[b, j, k].astype(F32)
            s1[b, j] = acc.astype(BF)
            if j < n - 1:
                send(s1.at[b, j], r2.at[b, j], (peers[j], z), f"second{b}")

    def second_sum(b):
        arrived(r2.at[b], f"second{b}")
        acc = s1[b, n - 1].astype(F32)
        for k in range(n - 1):
            acc = acc + r2[b, k].astype(F32)
        for i in range(width // CZ):
            s2[b // 2, b % 2 * (width // CZ) + i] = acc[:, i * CZ : (i + 1) * CZ].astype(BF)
        if b % 2 == 1:
            for k, place in enumerate(zs):
                send(s2.at[b // 2, place], r3.at[b // 2, k], (t, place), f"last{b // 2}")

    def last_sum(i):
        arrived(r3.at[i], f"last{i}")
        acc = s2[i, z].astype(F32)
        for k in range(nz - 1):
            acc = acc + r3[i, k].astype(F32)
        a2[i, z] = acc.astype(BF)
        for peer in zs:
            send(a2.at[i, z], a2.at[i, z], (t, peer), f"g_z{i}")

    def back_z(i):
        arrived(a2.at[i, pl.ds(0, nz - 1)], f"g_z{i}")
        for b in (2 * i, 2 * i + 1):
            _, v, peers, w = first_peers(b)
            mine = rows_of(c * R0 + v * R1 + w * R2, R2)
            for j in range(width // CZ):
                full_ref[b, mine, j * CZ : (j + 1) * CZ] = a2[i, b % 2 * (width // CZ) + j]
            strip = full_ref.at[b, mine]
            for k, peer in enumerate(peers):
                send(strip, strip, (peer, z), f"g_second{b}_{k}")
        for b in (2 * i, 2 * i + 1):
            pass_on(b, n - 1)

    def pass_on(b, k):
        peers, v, _, w = first_peers(b)
        place = plus(w, n - steps[k], n) if k < n - 1 else w
        strip = full_ref.at[b, rows_of(c * R0 + v * R1 + place * R2, R2)]
        for i, peer in enumerate(peers):
            send(strip, strip, (peer, z), f"g_first{b}_{i}")

    def back_second(b, k):
        arrived(s1.at[b, 0], f"g_second{b}_{k}")
        pass_on(b, k)

    def own_strip(b):
        strip = full_ref.at[b, strip_of(c, b, n - 1)]
        send(strip, strip, (partner, z), f"g_pair{b}_{n - 1}")

    def strip_of(core, b, k):
        _, v, _, _ = first_peers(b)
        place = plus(v, n - steps[k], n) if k < n - 1 else v
        return rows_of(core * R0 + place * R1, R1)

    def finish(core, b, k):
        strip = strip_of(core, b, k)
        gin_ref[strip, cols(b)] = full_ref[b, strip].astype(F32) * grad_scale

    def back_first(b, k):
        arrived(s1.at[b], f"g_first{b}_{k}")
        strip = full_ref.at[b, strip_of(c, b, k)]
        send(strip, strip, (partner, z), f"g_pair{b}_{k}")

    def back_pair(b, k):
        arrived(s1.at[b], f"g_pair{b}_{k}")
        finish(1 - c, b, k)

    d_gated = dg[...]
    g[4] = mm(gated, cot, TN).astype(BF)
    to_partner(4)
    normed_t = normed[...].T

    def weight_grad(b, d_proj):
        d = d_proj.astype(BF) * dsil[:, cols(b)]
        dpre[:, cols(b)] = d
        g[b] = mm(normed_t, d).astype(BF)
        to_partner(b)

    weight_grad(0, d_gated * nm)

    gn = d_gated * u32
    dm = inv_m * (
        gn - jnp.mean(gn, axis=1, keepdims=True) - nm * jnp.mean(gn * nm, axis=1, keepdims=True)
    )
    mixed[...] = dm
    d_v = []
    for i in range(HEADS // 2):
        dm_i = mixed[:, 128 * i : 128 * (i + 1)].astype(BF)
        part = None
        for j in range(2):
            term = mm(weights[2 * i + j], dm_i * side[j], TN)
            part = term if part is None else part + term
        d_v.append(part)
    pair_sum(4)
    weight_grad(1, jnp.concatenate(d_v, axis=1))

    d_q, d_k = [], []
    for i in range(HEADS // 2):
        q, k, v = pair(2, i), pair(3, i), pair(1, i)
        dm_i = mixed[:, 128 * i : 128 * (i + 1)].astype(BF)
        part_q = part_k = None
        for j in range(2):
            (ds,) = lower(
                lambda dw, factor: (dw.astype(BF) * factor,), mm(dm_i, v * side[j], NT), dfac[2 * i + j]
            )
            term_q = mm(ds, k * side[j])
            term_k = mm(ds, q * side[j], TN)
            part_q = term_q if part_q is None else part_q + term_q
            part_k = term_k if part_k is None else part_k + term_k
        d_q.append(part_q)
        d_k.append(part_k)
        if i == 0:
            pair_sum(0)
        if i == 2:
            pair_sum(1)
    weight_grad(2, jnp.concatenate(d_q, axis=1))
    weight_grad(3, jnp.concatenate(d_k, axis=1))
    pair_sum(2)
    pair_sum(3)

    out_ref[...] = (emb[...] + mm(gated_v[...], wout_v[...])).astype(BF)
    dn = mm(dpre[...], win_v[...], NT).astype(BF).astype(F32)
    nv = n32[...]
    de = cot.astype(F32) + inv_e * (
        dn - jnp.mean(dn, axis=1, keepdims=True) - nv * jnp.mean(dn * nv, axis=1, keepdims=True)
    )
    sg32 = mm(slot_hot, de.astype(BF))
    sg_s[...] = packed(sg32[:, :half], sg32[:, half:])
    sg_r[count - 1] = sg_s[t]

    RZ = R0 // nz
    CX = width // n
    orows = rows_of(c * R0 + z * RZ, RZ)
    ocols = rows_of(x * CX, CX)

    def out_z():
        arrived(ro1, "o_z")
        acc = h[4, rows_of(z * RZ, RZ)].astype(F32)
        for k in range(nz - 1):
            acc = acc + ro1[k].astype(F32)
        h[4, rows_of(z * RZ, RZ)] = acc.astype(BF)
        for k, (peer, place) in enumerate(zip(xs, plane(x))):
            send(
                h.at[4, rows_of(z * RZ, RZ), rows_of(place * CX, CX)], ro2.at[k], (peer, z), "o_x"
            )

    def out_x():
        arrived(ro2, "o_x")
        acc = h[4, rows_of(z * RZ, RZ), ocols].astype(F32)
        for k in range(n - 1):
            acc = acc + ro2[k].astype(F32)
        so2[...] = acc.astype(BF)
        ro3[y] = so2[...]
        for peer in ys:
            send(so2, ro3.at[y], (peer, z), "o_y")

    def out_y():
        arrived(ro3.at[pl.ds(0, n - 1)], "o_y")
        acc = ro3[0].astype(F32)
        for k in range(1, n):
            acc = acc + ro3[k].astype(F32)
        fullo_ref[orows, ocols] = acc.astype(BF)
        for peer in xs:
            strip = fullo_ref.at[orows, ocols]
            send(strip, strip, (peer, z), "o_gx")

    def out_back_x():
        arrived(ro2, "o_gx")
        for peer in zs:
            strip = fullo_ref.at[orows]
            send(strip, strip, (t, peer), "o_gz")

    def slots_out():
        for k, peer in enumerate(ahead):
            send(sg_s.at[peer], sg_r.at[k], (peer, z), "slot")

    for b in range(4):
        first_sum(b)
    for b in range(4):
        second_sum(b)
    out_z()
    slots_out()
    last_sum(0)
    out_x()
    last_sum(1)
    out_y()
    back_z(0)
    back_z(1)
    out_back_x()
    arrived(sg_r.at[pl.ds(0, count - 1)], "slot")
    tg_ref[...] = mm(row_hot[...], unpacked(sg_r), TN).astype(BF)
    for i in (0, 2):
        for k in reversed(range(n - 1)):
            back_second(i, k)
            back_second(i + 1, k)
        own_strip(i)
        own_strip(i + 1)
    for b in range(4):
        finish(c, b, n - 1)
    for k in reversed(range(n - 1)):
        back_first(0, k)
        back_first(1, k)
    arrived(ro1, "o_gz")
    strip = fullo_ref.at[own]
    send(strip, strip, (partner, z), "o_gp")
    for b in range(2):
        for k in range(n - 1):
            finish(c, b, k)
    gout_ref[own] = fullo_ref[own].astype(F32) * grad_scale
    for b in range(4):
        back_pair(b, n - 1)
    for k in reversed(range(n - 1)):
        back_pair(0, k)
        back_pair(1, k)
    for k in reversed(range(n - 1)):
        back_first(2, k)
        back_first(3, k)
        finish(c, 2, k)
        finish(c, 3, k)
    arrived(fullo_ref.at[other], "o_gp")
    gout_ref[other] = fullo_ref[other].astype(F32) * grad_scale
    for k in reversed(range(n - 1)):
        back_pair(2, k)
        back_pair(3, k)

    for ref, name in pending:
        pltpu.make_async_copy(ref, ref, send_sem.at[sem(name)]).wait()
    assert len(names) <= send_sem.shape[0]


def store(*refs):
    sems = refs[-1]
    copies = []
    for src, dst in zip(refs[:4], refs[4:8]):
        parts = 8 if src.dtype == F32 and src.shape[1] > src.shape[0] else 2
        size = src.shape[0] // parts
        for i in range(parts):
            part = pl.ds(i * size, size)
            copies.append(pltpu.make_async_copy(src.at[part], dst.at[part], sems.at[len(copies)]))
    for copy in copies:
        copy.start()
    for copy in copies:
        copy.wait()


def body(n, nz, table, fetch_rows, item_slot, seq_lengths, w_in, w_out, out_cot):
    _, count, cap = fetch_rows.shape
    rows, width = table.shape
    tokens = item_slot.shape[0]
    slots = count * cap
    half = width // 2
    R0 = width // 2
    R1 = R0 // n
    R2 = R1 // n
    CZ = 2 * width // nz
    any_ = pl.BlockSpec(memory_space=pl.ANY)
    vmem = pl.BlockSpec(memory_space=pltpu.VMEM)
    hbm = pl.BlockSpec(memory_space=pltpu.HBM)
    V = pltpu.VMEM
    grad_scale = float(tokens * count * nz) ** (-0.5)
    made = pl.pallas_call(
        functools.partial(kernel, n, nz, count, cap, rows, tokens, width, grad_scale),
        out_shape=(
            V((tokens, width), BF), V((rows, width), BF), V((width, 4 * width), F32), V((width, width), F32),
        ),
        in_specs=[hbm] * 7,
        out_specs=(vmem, vmem, vmem, vmem),
        scratch_shapes=[
            pltpu.SMEM((cap, count), jnp.int32), V((1, tokens), jnp.int32), pltpu.SMEM(seq_lengths.shape, jnp.int32),
            V((rows, width), BF), V((width, 4 * width), BF), V((width, width), BF), V((tokens, width), BF),
            V((count, 1, 128), jnp.int32), V((count, 1, 128), jnp.int32),
            V((count, 2 * cap, half), BF), V((count, 2 * cap, half), BF),
            V((count, 2 * cap, half), BF), V((count, 2 * cap, half), BF),
            V((slots, rows), BF), V((tokens, slots), BF), V((tokens, width), F32), V((tokens, width), BF), V((tokens, width), F32), V((tokens, width), F32), V((tokens, width), BF),
            V((tokens, 4 * width), BF), V((tokens, 4 * width), BF), V((tokens, 4 * width), BF),
            V((HEADS, tokens, tokens), BF), V((HEADS, tokens, tokens), BF),
            V((tokens, width), F32), V((tokens, tokens), BF),
            V((5, width, width), BF), V((5, R0, width), BF), V((5, R0, width), BF),
            V((4, n, n - 1, R2, width), BF), V((4, n, R2, width), BF),
            V((4, n - 1, R2, width), BF), V((2, nz, R2, CZ), BF),
            V((2, nz - 1, R2, CZ), BF), V((2, nz, R2, CZ), BF),
            V((nz - 1, R0 // nz, width), BF), V((n - 1, R0 // nz, width // n), BF),
            V((R0 // nz, width // n), BF), V((n, R0 // nz, width // n), BF),
            V((4, width, width), BF), V((width, width), BF),
            pltpu.SemaphoreType.DMA((7,)),
            pltpu.SemaphoreType.DMA((96,)),
            pltpu.SemaphoreType.DMA((96,)),
        ],
        compiler_params=pltpu.CompilerParams(
            collective_id=0, has_side_effects=True, vmem_limit_bytes=40 * 1024 * 1024
        ),
    )(
        *(
            pltpu.with_memory_space_constraint(v, pltpu.HBM)
            for v in (
                fetch_rows[0].T, item_slot.reshape(1, tokens), seq_lengths, table, w_in, w_out, out_cot
            )
        )
    )
    made = [pltpu.with_memory_space_constraint(v, pltpu.VMEM) for v in made]
    layer_out, table_grad, sum_in, sum_out = pl.pallas_call(
        store,
        out_shape=[jax.ShapeDtypeStruct(v.shape, v.dtype) for v in made],
        in_specs=[vmem] * 4,
        out_specs=[any_] * 4,
        scratch_shapes=[pltpu.SemaphoreType.DMA((16,))],
        compiler_params=pltpu.CompilerParams(vmem_limit_bytes=1024 * 1024),
    )(*made)
    return layer_out, table_grad[None], sum_in, sum_out


def solution(mesh):
    placed = (
        P("table", None),
        P(("table", "group"), None, None),
        P(("table", "group")),
        P(("table", "group"), None),
        P(),
        P(),
        P(("table", "group"), None),
    )
    n = math.isqrt(mesh.shape["table"] // 2)
    return jax.shard_map(
        functools.partial(body, n, mesh.shape["group"]),
        mesh=mesh,
        in_specs=placed,
        out_specs=(P(("table", "group"), None), P("group", "table", None), P(), P()),
        check_vma=False,
    )
```

```python
import functools
import math

import jax
import jax.numpy as jnp
from jax import lax
from jax.experimental import pallas as pl
from jax.experimental.pallas import tpu as pltpu
from jax.sharding import PartitionSpec as P

HEADS = 8
EPS = 1e-05
MESH = pl.DeviceIdType.MESH
BF = jnp.bfloat16
F32 = jnp.float32

NN = (((1,), (0,)), ((), ()))
NT = (((1,), (1,)), ((), ()))
TN = (((0,), (0,)), ((), ()))


def mm(a, b, dims=NN):
    return lax.dot_general(a, b, dims, preferred_element_type=F32)


def rows_of(start, size):
    return pl.ds(pl.multiple_of(start, size), size)


def kernel(
    n, nz, count, cap, rows, tokens, width, grad_scale,
    fetch_hbm, slot_hbm, len_hbm, table_hbm, win_hbm, wout_hbm, cot_hbm,
    out_ref, tg_ref, gin_ref, gout_ref,
    fetch_ref, slot_ref, len_ref, table_v, win_v, wout_v, cot_v,
    req_s, req_r, found, rows_r, sg_s, sg_r,
    row_hot, tok_hot, dg, gated_v, emb, n32, normed, proj, dsil, dpre, weights, dfac, mixed, allowed,
    g, pr, h, r1, s1, r2, s2, r3, a2,
    ro1, ro2, so2, ro3, full_ref, fullo_ref,
    load_sem, send_sem, recv_sem,
):
    t = lax.axis_index("table")
    z = lax.axis_index("group")
    x = lax.div(t, 2 * n)
    y = lax.rem(lax.div(t, 2), n)
    c = lax.rem(t, 2)
    slots = count * cap
    half = width // 2
    R0 = width // 2
    R1 = R0 // n
    R2 = R1 // n
    CZ = 2 * width // nz

    def at(px, py, pc):
        return (px * n + py) * 2 + pc

    def plus(v, d, m):
        return lax.rem(v + d, m)

    def far(d, m):
        return min(d, m - d)

    offsets = [(dx, dy, dc) for dx in range(n) for dy in range(n) for dc in range(2)][1:]
    offsets.sort(key=lambda o: (-far(o[0], n) - far(o[1], n), o))
    steps = sorted(range(1, n), key=lambda d: -far(d, n))
    zsteps = sorted(range(1, nz), key=lambda d: -far(d, nz))
    ahead = [at(plus(x, dx, n), plus(y, dy, n), plus(c, dc, 2)) for dx, dy, dc in offsets]
    behind = [at(plus(x, n - dx, n), plus(y, n - dy, n), plus(c, 2 - dc, 2)) for dx, dy, dc in offsets]
    zs = [plus(z, d, nz) for d in zsteps]
    xs = [at(plus(x, d, n), y, c) for d in steps]
    ys = [at(x, plus(y, d, n), c) for d in steps]
    partner = at(x, y, 1 - c)

    loads = [
        pltpu.make_async_copy(src, dst, load_sem.at[i])
        for i, (src, dst) in enumerate(
            (
                (fetch_hbm, fetch_ref), (len_hbm, len_ref), (slot_hbm, slot_ref),
                (table_hbm, table_v), (win_hbm, win_v), (wout_hbm, wout_v), (cot_hbm, cot_v),
            )
        )
    ]
    loads[0].start()
    barrier = pltpu.get_barrier_semaphore()
    for peer in ahead:
        pl.semaphore_signal(barrier, inc=1, device_id=(peer, z), device_id_type=MESH)
    for peer in zs:
        pl.semaphore_signal(barrier, inc=1, device_id=(t, peer), device_id_type=MESH)
    for copy in loads[1:]:
        copy.start()

    names = {}
    pending = []

    def sem(name):
        return names.setdefault(name, len(names))

    def send(src, dst, to, name):
        i = sem(name)
        pltpu.make_async_remote_copy(
            src_ref=src, dst_ref=dst, send_sem=send_sem.at[i], recv_sem=recv_sem.at[i],
            device_id=to, device_id_type=MESH,
        ).start()

    def arrived(ref, name):
        pltpu.make_async_copy(ref, ref, recv_sem.at[sem(name)]).wait()
        pending.append((ref, name))

    loads[0].wait()
    lane = lax.broadcasted_iota(jnp.int32, (1, 128), 1)
    for o in range(count):
        line = jnp.zeros((1, 128), jnp.int32)
        for e in range(cap):
            line = jnp.where(lane == e, fetch_ref[e, o], line)
        req_s[o] = line
    pl.semaphore_wait(barrier, count - 1 + nz - 1)
    for k, peer in enumerate(ahead):
        send(req_s.at[peer], req_r.at[k], (peer, z), f"list{0 if k < count // 2 else count // 2}")
    req_r[count - 1] = req_s[t]

    loads[1].wait()
    loads[2].wait()
    ends = []
    total = jnp.int32(0)
    for s in range(len_ref.shape[1]):
        total = total + len_ref[0, s]
        ends.append(total)
    pos_i = lax.broadcasted_iota(jnp.int32, (tokens, tokens), 0)
    pos_j = lax.broadcasted_iota(jnp.int32, (tokens, tokens), 1)
    first = jnp.zeros((tokens, tokens), jnp.int32)
    for e in ends:
        first = jnp.where(pos_i >= e, e, first)
    allowed[...] = jnp.where((pos_j >= first) & (pos_j <= pos_i), 1.0, 0.0).astype(BF)
    slot_hot = jnp.where(
        lax.broadcasted_iota(jnp.int32, (slots, tokens), 0) == slot_ref[...], 1.0, 0.0
    ).astype(BF)

    def hot_rows(start, size):
        lists = jnp.broadcast_to(req_r[start : start + size].astype(F32), (size, cap, 128))
        diagonal = lax.broadcasted_iota(jnp.int32, (size, cap, 128), 1) == lax.broadcasted_iota(
            jnp.int32, (size, cap, 128), 2
        )
        wanted = jnp.sum(jnp.where(diagonal, lists, 0.0), axis=2, keepdims=True).reshape(size * cap, 1)
        lane = lax.broadcasted_iota(jnp.int32, (size * cap, 128), 1).astype(F32)
        row_hot[start * cap : (start + size) * cap] = jnp.concatenate(
            [jnp.where(wanted == lane + 128.0 * i, 1.0, 0.0).astype(BF) for i in range(rows // 128)], axis=1
        )

    def packed(lo, hi):
        return jnp.concatenate([lo.reshape(-1, cap, half), hi.reshape(-1, cap, half)], axis=1).astype(BF)

    def unpacked(ref):
        v = ref[...].astype(F32)
        return jnp.concatenate(
            [v[:, :cap].reshape(slots, half), v[:, cap:].reshape(slots, half)], axis=1
        ).astype(BF)

    cut = count // 2
    for start, size, got in ((cut, cut, cut - 1), (0, cut, cut)):
        arrived(req_r.at[pl.ds(start, got)], f"list{start}")
        if start:
            loads[3].wait()
        hot_rows(start, size)
        hot = row_hot[start * cap : (start + size) * cap]
        found[start : start + size] = packed(mm(hot, table_v[:, :half]), mm(hot, table_v[:, half:]))
        for k in range(start, start + got):
            send(found.at[k], rows_r.at[t], (behind[k], z), "rows")
    rows_r[t] = found[count - 1]
    tok_hot[...] = slot_hot.T
    for i in (4, 5, 6):
        loads[i].wait()
    cot = cot_v[...]
    dg[...] = mm(cot, wout_v[...], NT).astype(BF).astype(F32)
    arrived(rows_r.at[pl.ds(0, count - 1)], "rows")

    e32 = mm(tok_hot[...], unpacked(rows_r))
    emb[...] = e32
    cen = e32 - jnp.mean(e32, axis=1, keepdims=True)
    inv_e = lax.rsqrt(jnp.mean(cen * cen, axis=1, keepdims=True) + EPS)
    n32[...] = cen * inv_e
    normed[...] = n32[...].astype(BF)

    def cols(b):
        return slice(b * width, (b + 1) * width)

    for b in range(4):
        p = mm(normed[...], win_v[:, cols(b)])
        sg = 0.5 + 0.5 * jnp.tanh(0.5 * p)
        act = p * sg
        proj[:, cols(b)] = act.astype(BF)
        dsil[:, cols(b)] = (sg + act * (1.0 - sg)).astype(BF)

    lanes = lax.broadcasted_iota(jnp.int32, (1, 128), 1)
    side = [
        jnp.where(lanes < 64, 1.0, 0.0).astype(BF),
        jnp.where(lanes >= 64, 1.0, 0.0).astype(BF),
    ]

    def pair(b, i):
        return proj[:, b * width + 128 * i : b * width + 128 * (i + 1)]

    scale = (width // HEADS) ** -0.5
    mid = tokens // 2

    def lower(f, *arrays):
        top = f(*(v[:mid, :mid] for v in arrays))
        low = f(*(v[mid:] for v in arrays))
        none = jnp.zeros((mid, tokens - mid), BF)
        return [
            jnp.concatenate([jnp.concatenate([a, none], axis=1), b], axis=0) for a, b in zip(top, low)
        ]

    def score(s, keep):
        sg = 0.5 + 0.5 * jnp.tanh((0.5 * scale) * s)
        act = (scale * s) * sg
        return act.astype(BF) * keep, (sg + act * (1.0 - sg)).astype(BF) * (keep * BF(scale))

    for i in range(HEADS // 2):
        q, k, v = pair(2, i), pair(3, i), pair(1, i)
        part = None
        for j in range(2):
            w, factor = lower(score, mm(q, k * side[j], NT), allowed[...])
            weights[2 * i + j] = w
            dfac[2 * i + j] = factor
            term = mm(w, v * side[j])
            part = term if part is None else part + term
        mixed[:, 128 * i : 128 * (i + 1)] = part

    m32 = mixed[...]
    cen = m32 - jnp.mean(m32, axis=1, keepdims=True)
    inv_m = lax.rsqrt(jnp.mean(cen * cen, axis=1, keepdims=True) + EPS)
    nm = cen * inv_m
    u32 = proj[:, cols(0)].astype(F32)
    gated = (nm * u32).astype(BF)
    gated_v[...] = gated

    own = rows_of(c * R0, R0)
    other = rows_of((1 - c) * R0, R0)

    def to_partner(b):
        send(g.at[b, other], pr.at[b], (partner, z), f"pair{b}")

    def first_peers(b):
        return (xs, x, ys, y) if b % 2 == 0 else (ys, y, xs, x)

    def plane(v):
        return [plus(v, d, n) for d in steps]

    def pair_sum(b):
        arrived(pr.at[b], f"pair{b}")
        h[b] = (g[b, own].astype(F32) + pr[b].astype(F32)).astype(BF)
        if b < 4:
            peers, v, _, w = first_peers(b)
            for j, sub in enumerate(plane(w) + [w]):
                for k, (peer, place) in enumerate(zip(peers, plane(v))):
                    send(h.at[b, rows_of(place * R1 + sub * R2, R2)], r1.at[b, j, k], (peer, z), f"first{b}_{j}")
        else:
            for k, place in enumerate(zs):
                send(h.at[b, rows_of(place * (R0 // nz), R0 // nz)], ro1.at[k], (t, place), "o_z")

    def first_sum(b):
        _, v, peers, w = first_peers(b)
        for j, sub in enumerate(plane(w) + [w]):
            arrived(r1.at[b, j], f"first{b}_{j}")
            acc = h[b, rows_of(v * R1 + sub * R2, R2)].astype(F32)
            for k in range(n - 1):
                acc = acc + r1[b, j, k].astype(F32)
            s1[b, j] = acc.astype(BF)
            if j < n - 1:
                send(s1.at[b, j], r2.at[b, j], (peers[j], z), f"second{b}")

    def second_sum(b):
        arrived(r2.at[b], f"second{b}")
        acc = s1[b, n - 1].astype(F32)
        for k in range(n - 1):
            acc = acc + r2[b, k].astype(F32)
        for i in range(width // CZ):
            s2[b // 2, b % 2 * (width // CZ) + i] = acc[:, i * CZ : (i + 1) * CZ].astype(BF)
        if b % 2 == 1:
            for k, place in enumerate(zs):
                send(s2.at[b // 2, place], r3.at[b // 2, k], (t, place), f"last{b // 2}")

    def last_sum(i):
        arrived(r3.at[i], f"last{i}")
        acc = s2[i, z].astype(F32)
        for k in range(nz - 1):
            acc = acc + r3[i, k].astype(F32)
        a2[i, z] = acc.astype(BF)
        for peer in zs:
            send(a2.at[i, z], a2.at[i, z], (t, peer), f"g_z{i}")

    def back_z(i):
        arrived(a2.at[i, pl.ds(0, nz - 1)], f"g_z{i}")
        for b in (2 * i, 2 * i + 1):
            _, v, peers, w = first_peers(b)
            mine = rows_of(c * R0 + v * R1 + w * R2, R2)
            for j in range(width // CZ):
                full_ref[b, mine, j * CZ : (j + 1) * CZ] = a2[i, b % 2 * (width // CZ) + j]
            strip = full_ref.at[b, mine]
            for k, peer in enumerate(peers):
                send(strip, strip, (peer, z), f"g_second{b}_{k}")
        for b in (2 * i, 2 * i + 1):
            pass_on(b, n - 1)

    def pass_on(b, k):
        peers, v, _, w = first_peers(b)
        place = plus(w, n - steps[k], n) if k < n - 1 else w
        strip = full_ref.at[b, rows_of(c * R0 + v * R1 + place * R2, R2)]
        for i, peer in enumerate(peers):
            send(strip, strip, (peer, z), f"g_first{b}_{i}")

    def back_second(b, k):
        arrived(s1.at[b, 0], f"g_second{b}_{k}")
        pass_on(b, k)

    def own_strip(b):
        strip = full_ref.at[b, strip_of(c, b, n - 1)]
        send(strip, strip, (partner, z), f"g_pair{b}_{n - 1}")

    def strip_of(core, b, k):
        _, v, _, _ = first_peers(b)
        place = plus(v, n - steps[k], n) if k < n - 1 else v
        return rows_of(core * R0 + place * R1, R1)

    def finish(core, b, k):
        strip = strip_of(core, b, k)
        gin_ref[strip, cols(b)] = full_ref[b, strip].astype(F32) * grad_scale

    def back_first(b, k):
        arrived(s1.at[b], f"g_first{b}_{k}")
        strip = full_ref.at[b, strip_of(c, b, k)]
        send(strip, strip, (partner, z), f"g_pair{b}_{k}")

    def back_pair(b, k):
        arrived(s1.at[b], f"g_pair{b}_{k}")
        finish(1 - c, b, k)

    d_gated = dg[...]
    g[4] = mm(gated, cot, TN).astype(BF)
    to_partner(4)
    normed_t = normed[...].T

    def weight_grad(b, d_proj):
        d = d_proj.astype(BF) * dsil[:, cols(b)]
        dpre[:, cols(b)] = d
        g[b] = mm(normed_t, d).astype(BF)
        to_partner(b)

    weight_grad(0, d_gated * nm)

    gn = d_gated * u32
    dm = inv_m * (
        gn - jnp.mean(gn, axis=1, keepdims=True) - nm * jnp.mean(gn * nm, axis=1, keepdims=True)
    )
    mixed[...] = dm
    d_v = []
    for i in range(HEADS // 2):
        dm_i = mixed[:, 128 * i : 128 * (i + 1)].astype(BF)
        part = None
        for j in range(2):
            term = mm(weights[2 * i + j], dm_i * side[j], TN)
            part = term if part is None else part + term
        d_v.append(part)
    pair_sum(4)
    weight_grad(1, jnp.concatenate(d_v, axis=1))

    d_q, d_k = [], []
    for i in range(HEADS // 2):
        q, k, v = pair(2, i), pair(3, i), pair(1, i)
        dm_i = mixed[:, 128 * i : 128 * (i + 1)].astype(BF)
        part_q = part_k = None
        for j in range(2):
            (ds,) = lower(
                lambda dw, factor: (dw.astype(BF) * factor,), mm(dm_i, v * side[j], NT), dfac[2 * i + j]
            )
            term_q = mm(ds, k * side[j])
            term_k = mm(ds, q * side[j], TN)
            part_q = term_q if part_q is None else part_q + term_q
            part_k = term_k if part_k is None else part_k + term_k
        d_q.append(part_q)
        d_k.append(part_k)
        if i == 0:
            pair_sum(0)
        if i == 2:
            pair_sum(1)
    weight_grad(2, jnp.concatenate(d_q, axis=1))
    weight_grad(3, jnp.concatenate(d_k, axis=1))
    pair_sum(2)
    pair_sum(3)

    out_ref[...] = (emb[...] + mm(gated_v[...], wout_v[...])).astype(BF)
    dn = mm(dpre[...], win_v[...], NT).astype(BF).astype(F32)
    nv = n32[...]
    de = cot.astype(F32) + inv_e * (
        dn - jnp.mean(dn, axis=1, keepdims=True) - nv * jnp.mean(dn * nv, axis=1, keepdims=True)
    )
    sg32 = mm(slot_hot, de.astype(BF))
    sg_s[...] = packed(sg32[:, :half], sg32[:, half:])
    sg_r[count - 1] = sg_s[t]

    RZ = R0 // nz
    CX = width // n
    orows = rows_of(c * R0 + z * RZ, RZ)
    ocols = rows_of(x * CX, CX)

    def out_z():
        arrived(ro1, "o_z")
        acc = h[4, rows_of(z * RZ, RZ)].astype(F32)
        for k in range(nz - 1):
            acc = acc + ro1[k].astype(F32)
        h[4, rows_of(z * RZ, RZ)] = acc.astype(BF)
        for k, (peer, place) in enumerate(zip(xs, plane(x))):
            send(
                h.at[4, rows_of(z * RZ, RZ), rows_of(place * CX, CX)], ro2.at[k], (peer, z), "o_x"
            )

    def out_x():
        arrived(ro2, "o_x")
        acc = h[4, rows_of(z * RZ, RZ), ocols].astype(F32)
        for k in range(n - 1):
            acc = acc + ro2[k].astype(F32)
        so2[...] = acc.astype(BF)
        ro3[y] = so2[...]
        for peer in ys:
            send(so2, ro3.at[y], (peer, z), "o_y")

    def out_y():
        arrived(ro3.at[pl.ds(0, n - 1)], "o_y")
        acc = ro3[0].astype(F32)
        for k in range(1, n):
            acc = acc + ro3[k].astype(F32)
        fullo_ref[orows, ocols] = acc.astype(BF)
        for peer in xs:
            strip = fullo_ref.at[orows, ocols]
            send(strip, strip, (peer, z), "o_gx")

    def out_back_x():
        arrived(ro2, "o_gx")
        for peer in zs:
            strip = fullo_ref.at[orows]
            send(strip, strip, (t, peer), "o_gz")

    def slots_out():
        for k, peer in enumerate(ahead):
            send(sg_s.at[peer], sg_r.at[k], (peer, z), "slot")

    for b in range(4):
        first_sum(b)
    for b in range(4):
        second_sum(b)
    out_z()
    slots_out()
    last_sum(0)
    out_x()
    last_sum(1)
    out_y()
    back_z(0)
    back_z(1)
    out_back_x()
    for i in (0, 2):
        for k in reversed(range(n - 1)):
            back_second(i, k)
            back_second(i + 1, k)
        own_strip(i)
        own_strip(i + 1)
        if i == 0:
            arrived(sg_r.at[pl.ds(0, count - 1)], "slot")
            tg_ref[...] = mm(row_hot[...], unpacked(sg_r), TN).astype(BF)
    for b in range(4):
        finish(c, b, n - 1)
    for k in reversed(range(n - 1)):
        back_first(0, k)
        back_first(1, k)
    arrived(ro1, "o_gz")
    strip = fullo_ref.at[own]
    send(strip, strip, (partner, z), "o_gp")
    for b in range(2):
        for k in range(n - 1):
            finish(c, b, k)
    gout_ref[own] = fullo_ref[own].astype(F32) * grad_scale
    for b in range(4):
        back_pair(b, n - 1)
    for k in reversed(range(n - 1)):
        back_pair(0, k)
        back_pair(1, k)
    for k in reversed(range(n - 1)):
        back_first(2, k)
        back_first(3, k)
        finish(c, 2, k)
        finish(c, 3, k)
    arrived(fullo_ref.at[other], "o_gp")
    gout_ref[other] = fullo_ref[other].astype(F32) * grad_scale
    for k in reversed(range(n - 1)):
        back_pair(2, k)
        back_pair(3, k)

    for ref, name in pending:
        pltpu.make_async_copy(ref, ref, send_sem.at[sem(name)]).wait()
    assert len(names) <= send_sem.shape[0]


def store(*refs):
    sems = refs[-1]
    copies = []
    for src, dst in zip(refs[:4], refs[4:8]):
        parts = 8 if src.dtype == F32 and src.shape[1] > src.shape[0] else 2
        size = src.shape[0] // parts
        for i in range(parts):
            part = pl.ds(i * size, size)
            copies.append(pltpu.make_async_copy(src.at[part], dst.at[part], sems.at[len(copies)]))
    for copy in copies:
        copy.start()
    for copy in copies:
        copy.wait()


def body(n, nz, table, fetch_rows, item_slot, seq_lengths, w_in, w_out, out_cot):
    _, count, cap = fetch_rows.shape
    rows, width = table.shape
    tokens = item_slot.shape[0]
    slots = count * cap
    half = width // 2
    R0 = width // 2
    R1 = R0 // n
    R2 = R1 // n
    CZ = 2 * width // nz
    any_ = pl.BlockSpec(memory_space=pl.ANY)
    vmem = pl.BlockSpec(memory_space=pltpu.VMEM)
    hbm = pl.BlockSpec(memory_space=pltpu.HBM)
    V = pltpu.VMEM
    grad_scale = float(tokens * count * nz) ** (-0.5)
    made = pl.pallas_call(
        functools.partial(kernel, n, nz, count, cap, rows, tokens, width, grad_scale),
        out_shape=(
            V((tokens, width), BF), V((rows, width), BF), V((width, 4 * width), F32), V((width, width), F32),
        ),
        in_specs=[hbm] * 7,
        out_specs=(vmem, vmem, vmem, vmem),
        scratch_shapes=[
            pltpu.SMEM((cap, count), jnp.int32), V((1, tokens), jnp.int32), pltpu.SMEM(seq_lengths.shape, jnp.int32),
            V((rows, width), BF), V((width, 4 * width), BF), V((width, width), BF), V((tokens, width), BF),
            V((count, 1, 128), jnp.int32), V((count, 1, 128), jnp.int32),
            V((count, 2 * cap, half), BF), V((count, 2 * cap, half), BF),
            V((count, 2 * cap, half), BF), V((count, 2 * cap, half), BF),
            V((slots, rows), BF), V((tokens, slots), BF), V((tokens, width), F32), V((tokens, width), BF), V((tokens, width), F32), V((tokens, width), F32), V((tokens, width), BF),
            V((tokens, 4 * width), BF), V((tokens, 4 * width), BF), V((tokens, 4 * width), BF),
            V((HEADS, tokens, tokens), BF), V((HEADS, tokens, tokens), BF),
            V((tokens, width), F32), V((tokens, tokens), BF),
            V((5, width, width), BF), V((5, R0, width), BF), V((5, R0, width), BF),
            V((4, n, n - 1, R2, width), BF), V((4, n, R2, width), BF),
            V((4, n - 1, R2, width), BF), V((2, nz, R2, CZ), BF),
            V((2, nz - 1, R2, CZ), BF), V((2, nz, R2, CZ), BF),
            V((nz - 1, R0 // nz, width), BF), V((n - 1, R0 // nz, width // n), BF),
            V((R0 // nz, width // n), BF), V((n, R0 // nz, width // n), BF),
            V((4, width, width), BF), V((width, width), BF),
            pltpu.SemaphoreType.DMA((7,)),
            pltpu.SemaphoreType.DMA((96,)),
            pltpu.SemaphoreType.DMA((96,)),
        ],
        compiler_params=pltpu.CompilerParams(
            collective_id=0, has_side_effects=True, vmem_limit_bytes=40 * 1024 * 1024
        ),
    )(
        *(
            pltpu.with_memory_space_constraint(v, pltpu.HBM)
            for v in (
                fetch_rows[0].T, item_slot.reshape(1, tokens), seq_lengths, table, w_in, w_out, out_cot
            )
        )
    )
    made = [pltpu.with_memory_space_constraint(v, pltpu.VMEM) for v in made]
    layer_out, table_grad, sum_in, sum_out = pl.pallas_call(
        store,
        out_shape=[jax.ShapeDtypeStruct(v.shape, v.dtype) for v in made],
        in_specs=[vmem] * 4,
        out_specs=[any_] * 4,
        scratch_shapes=[pltpu.SemaphoreType.DMA((16,))],
        compiler_params=pltpu.CompilerParams(vmem_limit_bytes=1024 * 1024),
    )(*made)
    return layer_out, table_grad[None], sum_in, sum_out


def solution(mesh):
    placed = (
        P("table", None),
        P(("table", "group"), None, None),
        P(("table", "group")),
        P(("table", "group"), None),
        P(),
        P(),
        P(("table", "group"), None),
    )
    n = math.isqrt(mesh.shape["table"] // 2)
    return jax.shard_map(
        functools.partial(body, n, mesh.shape["group"]),
        mesh=mesh,
        in_specs=placed,
        out_specs=(P(("table", "group"), None), P("group", "table", None), P(), P()),
        check_vma=False,
    )
```

```python
import functools
import math

import jax
import jax.numpy as jnp
from jax import lax
from jax.experimental import pallas as pl
from jax.experimental.pallas import tpu as pltpu
from jax.sharding import PartitionSpec as P

HEADS = 8
EPS = 1e-05
MESH = pl.DeviceIdType.MESH
BF = jnp.bfloat16
F32 = jnp.float32

NN = (((1,), (0,)), ((), ()))
NT = (((1,), (1,)), ((), ()))
TN = (((0,), (0,)), ((), ()))


def mm(a, b, dims=NN):
    return lax.dot_general(a, b, dims, preferred_element_type=F32)


def rows_of(start, size):
    return pl.ds(pl.multiple_of(start, size), size)


def kernel(
    n, nz, count, cap, rows, tokens, width, grad_scale,
    fetch_hbm, slot_hbm, len_hbm, table_hbm, win_hbm, wout_hbm, cot_hbm,
    out_ref, tg_ref, gin_ref, gout_ref,
    fetch_ref, slot_ref, len_ref, table_v, win_v, wout_v, cot_v,
    req_s, req_r, found, rows_r, sg_s, sg_r,
    row_hot, tok_hot, dg, gated_v, emb, n32, normed, proj, dsil, dpre, weights, dfac, mixed, allowed,
    g, pr, h, r1, s1, r2, s2, r3, a2,
    ro1, ro2, so2, ro3, full_ref, fullo_ref,
    load_sem, send_sem, recv_sem,
):
    t = lax.axis_index("table")
    z = lax.axis_index("group")
    x = lax.div(t, 2 * n)
    y = lax.rem(lax.div(t, 2), n)
    c = lax.rem(t, 2)
    slots = count * cap
    half = width // 2
    R0 = width // 2
    R1 = R0 // n
    R2 = R1 // n
    CZ = 2 * width // nz

    def at(px, py, pc):
        return (px * n + py) * 2 + pc

    def plus(v, d, m):
        return lax.rem(v + d, m)

    def far(d, m):
        return min(d, m - d)

    offsets = [(dx, dy, dc) for dx in range(n) for dy in range(n) for dc in range(2)][1:]
    offsets.sort(key=lambda o: (-far(o[0], n) - far(o[1], n), o))
    steps = sorted(range(1, n), key=lambda d: -far(d, n))
    zsteps = sorted(range(1, nz), key=lambda d: -far(d, nz))
    ahead = [at(plus(x, dx, n), plus(y, dy, n), plus(c, dc, 2)) for dx, dy, dc in offsets]
    behind = [at(plus(x, n - dx, n), plus(y, n - dy, n), plus(c, 2 - dc, 2)) for dx, dy, dc in offsets]
    zs = [plus(z, d, nz) for d in zsteps]
    xs = [at(plus(x, d, n), y, c) for d in steps]
    ys = [at(x, plus(y, d, n), c) for d in steps]
    partner = at(x, y, 1 - c)

    loads = [
        pltpu.make_async_copy(src, dst, load_sem.at[i])
        for i, (src, dst) in enumerate(
            (
                (fetch_hbm, fetch_ref), (len_hbm, len_ref), (slot_hbm, slot_ref),
                (table_hbm, table_v), (win_hbm, win_v), (wout_hbm, wout_v), (cot_hbm, cot_v),
            )
        )
    ]
    loads[0].start()
    barrier = pltpu.get_barrier_semaphore()
    for peer in ahead:
        pl.semaphore_signal(barrier, inc=1, device_id=(peer, z), device_id_type=MESH)
    for peer in zs:
        pl.semaphore_signal(barrier, inc=1, device_id=(t, peer), device_id_type=MESH)
    for copy in loads[1:]:
        copy.start()

    names = {}
    pending = []

    def sem(name):
        return names.setdefault(name, len(names))

    def send(src, dst, to, name):
        i = sem(name)
        pltpu.make_async_remote_copy(
            src_ref=src, dst_ref=dst, send_sem=send_sem.at[i], recv_sem=recv_sem.at[i],
            device_id=to, device_id_type=MESH,
        ).start()

    def arrived(ref, name):
        pltpu.make_async_copy(ref, ref, recv_sem.at[sem(name)]).wait()
        pending.append((ref, name))

    loads[0].wait()
    lane = lax.broadcasted_iota(jnp.int32, (1, 128), 1)
    for o in range(count):
        line = jnp.zeros((1, 128), jnp.int32)
        for e in range(cap):
            line = jnp.where(lane == e, fetch_ref[e, o], line)
        req_s[o] = line
    pl.semaphore_wait(barrier, count - 1 + nz - 1)
    for k, peer in enumerate(ahead):
        send(req_s.at[peer], req_r.at[k], (peer, z), f"list{0 if k < count // 2 else count // 2}")
    req_r[count - 1] = req_s[t]

    loads[1].wait()
    loads[2].wait()
    ends = []
    total = jnp.int32(0)
    for s in range(len_ref.shape[1]):
        total = total + len_ref[0, s]
        ends.append(total)
    pos_i = lax.broadcasted_iota(jnp.int32, (tokens, tokens), 0)
    pos_j = lax.broadcasted_iota(jnp.int32, (tokens, tokens), 1)
    first = jnp.zeros((tokens, tokens), jnp.int32)
    for e in ends:
        first = jnp.where(pos_i >= e, e, first)
    allowed[...] = jnp.where((pos_j >= first) & (pos_j <= pos_i), 1.0, 0.0).astype(BF)
    slot_hot = jnp.where(
        lax.broadcasted_iota(jnp.int32, (slots, tokens), 0) == slot_ref[...], 1.0, 0.0
    ).astype(BF)

    def hot_rows(start, size):
        lists = jnp.broadcast_to(req_r[start : start + size].astype(F32), (size, cap, 128))
        diagonal = lax.broadcasted_iota(jnp.int32, (size, cap, 128), 1) == lax.broadcasted_iota(
            jnp.int32, (size, cap, 128), 2
        )
        wanted = jnp.sum(jnp.where(diagonal, lists, 0.0), axis=2, keepdims=True).reshape(size * cap, 1)
        lane = lax.broadcasted_iota(jnp.int32, (size * cap, 128), 1).astype(F32)
        row_hot[start * cap : (start + size) * cap] = jnp.concatenate(
            [jnp.where(wanted == lane + 128.0 * i, 1.0, 0.0).astype(BF) for i in range(rows // 128)], axis=1
        )

    def packed(lo, hi):
        return jnp.concatenate([lo.reshape(-1, cap, half), hi.reshape(-1, cap, half)], axis=1).astype(BF)

    def unpacked(ref):
        v = ref[...].astype(F32)
        return jnp.concatenate(
            [v[:, :cap].reshape(slots, half), v[:, cap:].reshape(slots, half)], axis=1
        ).astype(BF)

    cut = count // 2
    for start, size, got in ((cut, cut, cut - 1), (0, cut, cut)):
        arrived(req_r.at[pl.ds(start, got)], f"list{start}")
        if start:
            loads[3].wait()
        hot_rows(start, size)
        hot = row_hot[start * cap : (start + size) * cap]
        found[start : start + size] = packed(mm(hot, table_v[:, :half]), mm(hot, table_v[:, half:]))
        for k in range(start, start + got):
            send(found.at[k], rows_r.at[t], (behind[k], z), "rows")
    rows_r[t] = found[count - 1]
    tok_hot[...] = slot_hot.T
    for i in (4, 5, 6):
        loads[i].wait()
    cot = cot_v[...]
    dg[...] = mm(cot, wout_v[...], NT).astype(BF).astype(F32)
    arrived(rows_r.at[pl.ds(0, count - 1)], "rows")

    e32 = mm(tok_hot[...], unpacked(rows_r))
    emb[...] = e32
    cen = e32 - jnp.mean(e32, axis=1, keepdims=True)
    inv_e = lax.rsqrt(jnp.mean(cen * cen, axis=1, keepdims=True) + EPS)
    n32[...] = cen * inv_e
    normed[...] = n32[...].astype(BF)

    def cols(b):
        return slice(b * width, (b + 1) * width)

    for b in range(4):
        p = mm(normed[...], win_v[:, cols(b)])
        sg = 0.5 + 0.5 * jnp.tanh(0.5 * p)
        act = p * sg
        proj[:, cols(b)] = act.astype(BF)
        dsil[:, cols(b)] = (sg + act * (1.0 - sg)).astype(BF)

    lanes = lax.broadcasted_iota(jnp.int32, (1, 128), 1)
    side = [
        jnp.where(lanes < 64, 1.0, 0.0).astype(BF),
        jnp.where(lanes >= 64, 1.0, 0.0).astype(BF),
    ]

    def pair(b, i):
        return proj[:, b * width + 128 * i : b * width + 128 * (i + 1)]

    scale = (width // HEADS) ** -0.5
    mid = tokens // 2

    def lower(f, *arrays):
        top = f(*(v[:mid, :mid] for v in arrays))
        low = f(*(v[mid:] for v in arrays))
        none = jnp.zeros((mid, tokens - mid), BF)
        return [
            jnp.concatenate([jnp.concatenate([a, none], axis=1), b], axis=0) for a, b in zip(top, low)
        ]

    def score(s, keep):
        sg = 0.5 + 0.5 * jnp.tanh((0.5 * scale) * s)
        act = (scale * s) * sg
        return act.astype(BF) * keep, (sg + act * (1.0 - sg)).astype(BF) * (keep * BF(scale))

    for i in range(HEADS // 2):
        q, k, v = pair(2, i), pair(3, i), pair(1, i)
        part = None
        for j in range(2):
            w, factor = lower(score, mm(q, k * side[j], NT), allowed[...])
            weights[2 * i + j] = w
            dfac[2 * i + j] = factor
            term = mm(w, v * side[j])
            part = term if part is None else part + term
        mixed[:, 128 * i : 128 * (i + 1)] = part

    m32 = mixed[...]
    cen = m32 - jnp.mean(m32, axis=1, keepdims=True)
    inv_m = lax.rsqrt(jnp.mean(cen * cen, axis=1, keepdims=True) + EPS)
    nm = cen * inv_m
    u32 = proj[:, cols(0)].astype(F32)
    gated = (nm * u32).astype(BF)
    gated_v[...] = gated

    own = rows_of(c * R0, R0)
    other = rows_of((1 - c) * R0, R0)

    def to_partner(b):
        send(g.at[b, other], pr.at[b], (partner, z), f"pair{b}")

    def first_peers(b):
        return (xs, x, ys, y) if b % 2 == 0 else (ys, y, xs, x)

    def plane(v):
        return [plus(v, d, n) for d in steps]

    def pair_sum(b):
        arrived(pr.at[b], f"pair{b}")
        h[b] = (g[b, own].astype(F32) + pr[b].astype(F32)).astype(BF)
        if b < 4:
            peers, v, _, w = first_peers(b)
            for j, sub in enumerate(plane(w) + [w]):
                for k, (peer, place) in enumerate(zip(peers, plane(v))):
                    send(h.at[b, rows_of(place * R1 + sub * R2, R2)], r1.at[b, j, k], (peer, z), f"first{b}_{j}")
        else:
            for k, place in enumerate(zs):
                send(h.at[b, rows_of(place * (R0 // nz), R0 // nz)], ro1.at[k], (t, place), "o_z")

    def first_sum(b):
        _, v, peers, w = first_peers(b)
        for j, sub in enumerate(plane(w) + [w]):
            arrived(r1.at[b, j], f"first{b}_{j}")
            acc = h[b, rows_of(v * R1 + sub * R2, R2)].astype(F32)
            for k in range(n - 1):
                acc = acc + r1[b, j, k].astype(F32)
            s1[b, j] = acc.astype(BF)
            if j < n - 1:
                send(s1.at[b, j], r2.at[b, j], (peers[j], z), f"second{b}")

    def second_sum(b):
        arrived(r2.at[b], f"second{b}")
        acc = s1[b, n - 1].astype(F32)
        for k in range(n - 1):
            acc = acc + r2[b, k].astype(F32)
        for i in range(width // CZ):
            s2[b // 2, b % 2 * (width // CZ) + i] = acc[:, i * CZ : (i + 1) * CZ].astype(BF)
        if b % 2 == 1:
            for k, place in enumerate(zs):
                send(s2.at[b // 2, place], r3.at[b // 2, k], (t, place), f"last{b // 2}")

    def last_sum(i):
        arrived(r3.at[i], f"last{i}")
        acc = s2[i, z].astype(F32)
        for k in range(nz - 1):
            acc = acc + r3[i, k].astype(F32)
        a2[i, z] = acc.astype(BF)
        for peer in zs:
            send(a2.at[i, z], a2.at[i, z], (t, peer), f"g_z{i}")

    def back_z(i):
        arrived(a2.at[i, pl.ds(0, nz - 1)], f"g_z{i}")
        for b in (2 * i, 2 * i + 1):
            _, v, peers, w = first_peers(b)
            mine = rows_of(c * R0 + v * R1 + w * R2, R2)
            for j in range(width // CZ):
                full_ref[b, mine, j * CZ : (j + 1) * CZ] = a2[i, b % 2 * (width // CZ) + j]
            strip = full_ref.at[b, mine]
            for k, peer in enumerate(peers):
                send(strip, strip, (peer, z), f"g_second{b}_{k}")
        for b in (2 * i, 2 * i + 1):
            pass_on(b, n - 1)

    def pass_on(b, k):
        peers, v, _, w = first_peers(b)
        place = plus(w, n - steps[k], n) if k < n - 1 else w
        strip = full_ref.at[b, rows_of(c * R0 + v * R1 + place * R2, R2)]
        for i, peer in enumerate(peers):
            send(strip, strip, (peer, z), f"g_first{b}_{i}")

    def back_second(b, k):
        arrived(s1.at[b, 0], f"g_second{b}_{k}")
        pass_on(b, k)

    def own_strip(b):
        strip = full_ref.at[b, strip_of(c, b, n - 1)]
        send(strip, strip, (partner, z), f"g_pair{b}_{n - 1}")

    def strip_of(core, b, k):
        _, v, _, _ = first_peers(b)
        place = plus(v, n - steps[k], n) if k < n - 1 else v
        return rows_of(core * R0 + place * R1, R1)

    def finish(core, b, k):
        strip = strip_of(core, b, k)
        gin_ref[strip, cols(b)] = full_ref[b, strip].astype(F32) * grad_scale

    def back_first(b, k):
        arrived(s1.at[b], f"g_first{b}_{k}")
        strip = full_ref.at[b, strip_of(c, b, k)]
        send(strip, strip, (partner, z), f"g_pair{b}_{k}")

    def back_pair(b, k):
        arrived(s1.at[b], f"g_pair{b}_{k}")
        finish(1 - c, b, k)

    d_gated = dg[...]
    g[4] = mm(gated, cot, TN).astype(BF)
    to_partner(4)
    normed_t = normed[...].T

    def weight_grad(b, d_proj):
        d = d_proj.astype(BF) * dsil[:, cols(b)]
        dpre[:, cols(b)] = d
        g[b] = mm(normed_t, d).astype(BF)
        to_partner(b)

    weight_grad(0, d_gated * nm)

    gn = d_gated * u32
    dm = inv_m * (
        gn - jnp.mean(gn, axis=1, keepdims=True) - nm * jnp.mean(gn * nm, axis=1, keepdims=True)
    )
    mixed[...] = dm
    d_v = []
    for i in range(HEADS // 2):
        dm_i = mixed[:, 128 * i : 128 * (i + 1)].astype(BF)
        part = None
        for j in range(2):
            term = mm(weights[2 * i + j], dm_i * side[j], TN)
            part = term if part is None else part + term
        d_v.append(part)
    pair_sum(4)
    weight_grad(1, jnp.concatenate(d_v, axis=1))

    d_q, d_k = [], []
    for i in range(HEADS // 2):
        q, k, v = pair(2, i), pair(3, i), pair(1, i)
        dm_i = mixed[:, 128 * i : 128 * (i + 1)].astype(BF)
        part_q = part_k = None
        for j in range(2):
            (ds,) = lower(
                lambda dw, factor: (dw.astype(BF) * factor,), mm(dm_i, v * side[j], NT), dfac[2 * i + j]
            )
            term_q = mm(ds, k * side[j])
            term_k = mm(ds, q * side[j], TN)
            part_q = term_q if part_q is None else part_q + term_q
            part_k = term_k if part_k is None else part_k + term_k
        d_q.append(part_q)
        d_k.append(part_k)
        if i == 0:
            pair_sum(0)
        if i == 1:
            pair_sum(1)
    weight_grad(2, jnp.concatenate(d_q, axis=1))
    weight_grad(3, jnp.concatenate(d_k, axis=1))
    pair_sum(2)
    pair_sum(3)

    out_ref[...] = (emb[...] + mm(gated_v[...], wout_v[...])).astype(BF)
    dn = mm(dpre[...], win_v[...], NT).astype(BF).astype(F32)
    nv = n32[...]
    de = cot.astype(F32) + inv_e * (
        dn - jnp.mean(dn, axis=1, keepdims=True) - nv * jnp.mean(dn * nv, axis=1, keepdims=True)
    )
    sg32 = mm(slot_hot, de.astype(BF))
    sg_s[...] = packed(sg32[:, :half], sg32[:, half:])
    sg_r[count - 1] = sg_s[t]

    RZ = R0 // nz
    CX = width // n
    orows = rows_of(c * R0 + z * RZ, RZ)
    ocols = rows_of(x * CX, CX)

    def out_z():
        arrived(ro1, "o_z")
        acc = h[4, rows_of(z * RZ, RZ)].astype(F32)
        for k in range(nz - 1):
            acc = acc + ro1[k].astype(F32)
        h[4, rows_of(z * RZ, RZ)] = acc.astype(BF)
        for k, (peer, place) in enumerate(zip(xs, plane(x))):
            send(
                h.at[4, rows_of(z * RZ, RZ), rows_of(place * CX, CX)], ro2.at[k], (peer, z), "o_x"
            )

    def out_x():
        arrived(ro2, "o_x")
        acc = h[4, rows_of(z * RZ, RZ), ocols].astype(F32)
        for k in range(n - 1):
            acc = acc + ro2[k].astype(F32)
        so2[...] = acc.astype(BF)
        ro3[y] = so2[...]
        for peer in ys:
            send(so2, ro3.at[y], (peer, z), "o_y")

    def out_y():
        arrived(ro3.at[pl.ds(0, n - 1)], "o_y")
        acc = ro3[0].astype(F32)
        for k in range(1, n):
            acc = acc + ro3[k].astype(F32)
        fullo_ref[orows, ocols] = acc.astype(BF)
        for peer in xs:
            strip = fullo_ref.at[orows, ocols]
            send(strip, strip, (peer, z), "o_gx")

    def out_back_x():
        arrived(ro2, "o_gx")
        for peer in zs:
            strip = fullo_ref.at[orows]
            send(strip, strip, (t, peer), "o_gz")

    def slots_out():
        for k, peer in enumerate(ahead):
            send(sg_s.at[peer], sg_r.at[k], (peer, z), "slot")

    for b in range(4):
        first_sum(b)
    for b in range(4):
        second_sum(b)
    out_z()
    slots_out()
    last_sum(0)
    out_x()
    last_sum(1)
    out_y()
    back_z(0)
    back_z(1)
    out_back_x()
    arrived(sg_r.at[pl.ds(0, count - 1)], "slot")
    tg_ref[...] = mm(row_hot[...], unpacked(sg_r), TN).astype(BF)
    for i in (0, 2):
        for k in reversed(range(n - 1)):
            back_second(i, k)
            back_second(i + 1, k)
        own_strip(i)
        own_strip(i + 1)
    for b in range(4):
        finish(c, b, n - 1)
    for k in reversed(range(n - 1)):
        back_first(0, k)
        back_first(1, k)
    arrived(ro1, "o_gz")
    strip = fullo_ref.at[own]
    send(strip, strip, (partner, z), "o_gp")
    for b in range(2):
        for k in range(n - 1):
            finish(c, b, k)
    gout_ref[own] = fullo_ref[own].astype(F32) * grad_scale
    for b in range(4):
        back_pair(b, n - 1)
    for k in reversed(range(n - 1)):
        back_pair(0, k)
        back_pair(1, k)
    for k in reversed(range(n - 1)):
        back_first(2, k)
        back_first(3, k)
        finish(c, 2, k)
        finish(c, 3, k)
    arrived(fullo_ref.at[other], "o_gp")
    gout_ref[other] = fullo_ref[other].astype(F32) * grad_scale
    for k in reversed(range(n - 1)):
        back_pair(2, k)
        back_pair(3, k)

    for ref, name in pending:
        pltpu.make_async_copy(ref, ref, send_sem.at[sem(name)]).wait()
    assert len(names) <= send_sem.shape[0]


def store(*refs):
    sems = refs[-1]
    copies = []
    for src, dst in zip(refs[:4], refs[4:8]):
        parts = 8 if src.dtype == F32 and src.shape[1] > src.shape[0] else 2
        size = src.shape[0] // parts
        for i in range(parts):
            part = pl.ds(i * size, size)
            copies.append(pltpu.make_async_copy(src.at[part], dst.at[part], sems.at[len(copies)]))
    for copy in copies:
        copy.start()
    for copy in copies:
        copy.wait()


def body(n, nz, table, fetch_rows, item_slot, seq_lengths, w_in, w_out, out_cot):
    _, count, cap = fetch_rows.shape
    rows, width = table.shape
    tokens = item_slot.shape[0]
    slots = count * cap
    half = width // 2
    R0 = width // 2
    R1 = R0 // n
    R2 = R1 // n
    CZ = 2 * width // nz
    any_ = pl.BlockSpec(memory_space=pl.ANY)
    vmem = pl.BlockSpec(memory_space=pltpu.VMEM)
    hbm = pl.BlockSpec(memory_space=pltpu.HBM)
    V = pltpu.VMEM
    grad_scale = float(tokens * count * nz) ** (-0.5)
    made = pl.pallas_call(
        functools.partial(kernel, n, nz, count, cap, rows, tokens, width, grad_scale),
        out_shape=(
            V((tokens, width), BF), V((rows, width), BF), V((width, 4 * width), F32), V((width, width), F32),
        ),
        in_specs=[hbm] * 7,
        out_specs=(vmem, vmem, vmem, vmem),
        scratch_shapes=[
            pltpu.SMEM((cap, count), jnp.int32), V((1, tokens), jnp.int32), pltpu.SMEM(seq_lengths.shape, jnp.int32),
            V((rows, width), BF), V((width, 4 * width), BF), V((width, width), BF), V((tokens, width), BF),
            V((count, 1, 128), jnp.int32), V((count, 1, 128), jnp.int32),
            V((count, 2 * cap, half), BF), V((count, 2 * cap, half), BF),
            V((count, 2 * cap, half), BF), V((count, 2 * cap, half), BF),
            V((slots, rows), BF), V((tokens, slots), BF), V((tokens, width), F32), V((tokens, width), BF), V((tokens, width), F32), V((tokens, width), F32), V((tokens, width), BF),
            V((tokens, 4 * width), BF), V((tokens, 4 * width), BF), V((tokens, 4 * width), BF),
            V((HEADS, tokens, tokens), BF), V((HEADS, tokens, tokens), BF),
            V((tokens, width), F32), V((tokens, tokens), BF),
            V((5, width, width), BF), V((5, R0, width), BF), V((5, R0, width), BF),
            V((4, n, n - 1, R2, width), BF), V((4, n, R2, width), BF),
            V((4, n - 1, R2, width), BF), V((2, nz, R2, CZ), BF),
            V((2, nz - 1, R2, CZ), BF), V((2, nz, R2, CZ), BF),
            V((nz - 1, R0 // nz, width), BF), V((n - 1, R0 // nz, width // n), BF),
            V((R0 // nz, width // n), BF), V((n, R0 // nz, width // n), BF),
            V((4, width, width), BF), V((width, width), BF),
            pltpu.SemaphoreType.DMA((7,)),
            pltpu.SemaphoreType.DMA((96,)),
            pltpu.SemaphoreType.DMA((96,)),
        ],
        compiler_params=pltpu.CompilerParams(
            collective_id=0, has_side_effects=True, vmem_limit_bytes=40 * 1024 * 1024
        ),
    )(
        *(
            pltpu.with_memory_space_constraint(v, pltpu.HBM)
            for v in (
                fetch_rows[0].T, item_slot.reshape(1, tokens), seq_lengths, table, w_in, w_out, out_cot
            )
        )
    )
    made = [pltpu.with_memory_space_constraint(v, pltpu.VMEM) for v in made]
    layer_out, table_grad, sum_in, sum_out = pl.pallas_call(
        store,
        out_shape=[jax.ShapeDtypeStruct(v.shape, v.dtype) for v in made],
        in_specs=[vmem] * 4,
        out_specs=[any_] * 4,
        scratch_shapes=[pltpu.SemaphoreType.DMA((16,))],
        compiler_params=pltpu.CompilerParams(vmem_limit_bytes=1024 * 1024),
    )(*made)
    return layer_out, table_grad[None], sum_in, sum_out


def solution(mesh):
    placed = (
        P("table", None),
        P(("table", "group"), None, None),
        P(("table", "group")),
        P(("table", "group"), None),
        P(),
        P(),
        P(("table", "group"), None),
    )
    n = math.isqrt(mesh.shape["table"] // 2)
    return jax.shard_map(
        functools.partial(body, n, mesh.shape["group"]),
        mesh=mesh,
        in_specs=placed,
        out_specs=(P(("table", "group"), None), P("group", "table", None), P(), P()),
        check_vma=False,
    )
```
